128 devices in a mesh: src: 16 (over y, x), obs: 8 (over z, core).
Axes of the slice: x: 4, y: 4, z: 4, core: 2. Of those that a mesh axis runs over, the one named last changes fastest.
Arguments:
- history: bfloat16 [8, 128, 256, 128], P(None, 'src'), may hold values from -6 to 6
- tiles: bfloat16 [8192, 256, 256], P(('src', 'obs')), may hold values from -0.0390625 to 0.0390625
- tile_obs: int32 [8192], P(('src', 'obs')), may hold values from 0 to 15
- tile_src: int32 [8192], P(('src', 'obs')), may hold values from 0 to 7
- tile_lag: int32 [8192], P(('src', 'obs')), may hold values from 1 to 8
- help_tiles: bfloat16 [3072, 256, 256], P(('src', 'obs')), may hold values from -0.0390625 to 0.0390625
- help_obs: int32 [3072], P(('src', 'obs')), may hold values from 0 to 15
- help_src: int32 [3072], replicated, may hold values from 0 to 127, as said below
- help_lag: int32 [3072], replicated, may hold values from 4 to 8
- self_inverse: float32 [128, 256, 256], P(('src', 'obs')), may hold values from -0.375 to 0.375
- excitation: bfloat16 [4, 128, 256, 128], P(None, ('src', 'obs')), may hold values from -6 to 6
Outputs:
- currents: bfloat16 [4, 128, 256, 128], P(None, ('src', 'obs'))
The draws below stay inside these ranges and needn't reach their ends.
Inputs may be any that keep to these rules, and one draw needn't show every extreme that they name: `help_src`: each device's block of 24 entries names source groups outside the device's own source row; at most 4 of them lie in any one source row, and exactly 4 in some row.
All inputs are finite; a program needn't handle non-finite values.
Results may differ from the reference program's by a relative error of at most 0.003.
Values may be sent and summed in bfloat16 or wider, within the bound.
A program may use at most 192 MiB of HBM per device.

```python
import jax
import jax.numpy as jnp
from jax import lax

G = 256
RHS = 128
LAGS = 8
STEPS = 4
GS_DEV = 1
TILE_DEV = 64
HELP_DEV = 24
CAP = 4
SG = 8
OG = 16
NG = 128
N_SRC = 16
N_OBS = 8


def draw_help_src(key, part):
    key = jax.random.fold_in(key, 11)
    devices = N_SRC * N_OBS

    def one_device(dev_key, dev):
        row = dev // N_OBS
        key_first, key_order, key_local = jax.random.split(dev_key, 3)
        others = (row + 1 + jnp.arange(N_SRC - 1, dtype=jnp.int32)) % N_SRC
        first = jax.random.randint(key_first, (), 0, N_SRC - 1)
        slot_rows = jnp.repeat(jnp.arange(N_SRC - 1, dtype=jnp.int32), CAP)
        scores = jax.random.permutation(key_order, (N_SRC - 1) * CAP).astype(jnp.int32) + 1
        scores = jnp.where(slot_rows == first, 0, scores)
        order = jnp.argsort(scores, stable=True)
        chosen = others[slot_rows[order[:HELP_DEV]]]
        local = jax.random.randint(key_local, (HELP_DEV,), 0, SG)
        return (chosen * SG + local).astype(jnp.int32)
    keys = jax.random.split(key, devices)
    return jax.vmap(one_device)(keys, jnp.arange(devices, dtype=jnp.int32)).reshape(-1).astype(jnp.int32)


def touch_ends(result, key, smallest, high):
    dims = result.shape
    spot = [jax.random.randint(jax.random.fold_in(key, axis), (), 0, dims[axis]) for axis in range(len(dims))]
    result = result.at[tuple(spot)].set(smallest)
    longest = dims.index(max(dims))
    spot[longest] = (spot[longest] + 1) % dims[longest]
    return result.at[tuple(spot)].set(high)


def block_scale(key, extent, cuts, smallest, high):
    loudness, own = 1.0, jax.random.fold_in(key, 6)
    for axis_at, parts in cuts:
        steps = jnp.exp(jax.random.uniform(jax.random.fold_in(own, axis_at), (parts,), jnp.float32, smallest / len(cuts), high / len(cuts)))
        loudness = loudness * jnp.repeat(steps, extent[axis_at] // parts).reshape([-1 if axis == axis_at else 1 for axis in range(len(extent))])
    return loudness


def normal_values(rng, extent, spread, most, pieces=(), kind=jnp.bfloat16):
    values = spread * jax.random.normal(rng, extent, jnp.float32)
    if pieces:
        values = values * block_scale(rng, extent, pieces, -0.22, 0.18)
    return jnp.clip(values, -most, most).astype(kind)


def setup_inputs(seed: int = 0) -> dict:
    splits = jax.random.split(jax.random.key(seed), 12)
    history = normal_values(splits[0], (LAGS, NG, G, RHS), 1.0, 6.0, ((1, 16),))
    tiles = normal_values(splits[1], (N_SRC * N_OBS * TILE_DEV, G, G), (G * (TILE_DEV + HELP_DEV) // GS_DEV) ** -0.5, 0.0390625, ((0, 128),))
    tile_obs = touch_ends(jax.random.randint(splits[2], (N_SRC * N_OBS * TILE_DEV,), 0, OG), jax.random.fold_in(splits[2], 1), 0, OG - 1).astype(jnp.int32)
    tile_src = touch_ends(jax.random.randint(splits[3], (N_SRC * N_OBS * TILE_DEV,), 0, SG), jax.random.fold_in(splits[3], 1), 0, SG - 1).astype(jnp.int32)
    tile_lag = touch_ends(jax.random.randint(splits[4], (N_SRC * N_OBS * TILE_DEV,), 1, LAGS + 1), jax.random.fold_in(splits[4], 1), 1, LAGS).astype(jnp.int32)
    help_tiles = normal_values(splits[5], (N_SRC * N_OBS * HELP_DEV, G, G), (G * (TILE_DEV + HELP_DEV) // GS_DEV) ** -0.5, 0.0390625, ((0, 128),))
    help_obs = touch_ends(jax.random.randint(splits[6], (N_SRC * N_OBS * HELP_DEV,), 0, OG), jax.random.fold_in(splits[6], 1), 0, OG - 1).astype(jnp.int32)
    help_src = draw_help_src(jax.random.fold_in(splits[11], 71), 0)
    help_lag = touch_ends(jax.random.randint(splits[8], (N_SRC * N_OBS * HELP_DEV,), STEPS, LAGS + 1), jax.random.fold_in(splits[8], 1), STEPS, LAGS).astype(jnp.int32)
    self_inverse = normal_values(splits[9], (NG, G, G), G ** -0.5, 0.375, ((0, 128),), jnp.float32)
    excitation = normal_values(splits[10], (STEPS, NG, G, RHS), 1.0, 6.0, ((1, 128),))
    return {"history": history, "tiles": tiles, "tile_obs": tile_obs, "tile_src": tile_src, "tile_lag": tile_lag, "help_tiles": help_tiles, "help_obs": help_obs, "help_src": help_src, "help_lag": help_lag, "self_inverse": self_inverse, "excitation": excitation}


def reference(history, tiles, tile_obs, tile_src, tile_lag, help_tiles, help_obs, help_src, help_lag, self_inverse, excitation):
    n_dev = N_SRC * N_OBS
    own_z = tiles.reshape(n_dev, TILE_DEV, G, G)
    own_obs = tile_obs.reshape(n_dev, TILE_DEV)
    own_src = tile_src.reshape(n_dev, TILE_DEV)
    own_lag = tile_lag.reshape(n_dev, TILE_DEV)
    aid_z = help_tiles.reshape(n_dev, HELP_DEV, G, G)
    aid_obs = help_obs.reshape(n_dev, HELP_DEV)
    aid_src = help_src.reshape(n_dev, HELP_DEV)
    aid_lag = help_lag.reshape(n_dev, HELP_DEV)
    slab_ids = jnp.arange(OG, dtype=jnp.int32)
    currents = jnp.zeros((STEPS, NG, G, RHS), jnp.bfloat16)
    for step in range(STEPS):
        table = jnp.concatenate([history, currents], axis=0).reshape(((LAGS + STEPS) * NG, G, RHS))

        def device_field(carry, dev):
            row = dev // N_OBS
            col = dev % N_OBS
            z_own = lax.dynamic_index_in_dim(own_z, dev, 0, keepdims=False)
            obs_own = lax.dynamic_index_in_dim(own_obs, dev, 0, keepdims=False)
            src_own = row * SG + lax.dynamic_index_in_dim(own_src, dev, 0, keepdims=False)
            lag_own = lax.dynamic_index_in_dim(own_lag, dev, 0, keepdims=False)
            z_aid = lax.dynamic_index_in_dim(aid_z, dev, 0, keepdims=False)
            obs_aid = lax.dynamic_index_in_dim(aid_obs, dev, 0, keepdims=False)
            src_aid = lax.dynamic_index_in_dim(aid_src, dev, 0, keepdims=False)
            lag_aid = lax.dynamic_index_in_dim(aid_lag, dev, 0, keepdims=False)
            z_all = jnp.concatenate([z_own, z_aid], axis=0).astype(jnp.float32)
            obs_all = jnp.concatenate([obs_own, obs_aid], axis=0)
            src_all = jnp.concatenate([src_own, src_aid], axis=0)
            lag_all = jnp.concatenate([lag_own, lag_aid], axis=0)
            index = ((LAGS + step - lag_all) * NG + src_all).astype(jnp.int32)
            picked = jnp.take(table, index, axis=0).astype(jnp.float32)
            prod = jnp.einsum('tab,tbr->tar', z_all, picked)
            onehot = (obs_all[None, :] == slab_ids[:, None]).astype(jnp.float32)
            slab = jnp.dot(onehot, prod.reshape(prod.shape[0], G * RHS), precision=lax.Precision.HIGHEST)
            current = lax.dynamic_index_in_dim(carry, col, 0, keepdims=False)
            carry = lax.dynamic_update_index_in_dim(carry, current + slab.reshape(OG, G, RHS), col, 0)
            return carry, None

        start = jnp.zeros((N_OBS, OG, G, RHS), jnp.float32)
        columns, _ = lax.scan(device_field, start, jnp.arange(n_dev, dtype=jnp.int32))
        field = columns.reshape(N_OBS, N_SRC, GS_DEV, G, RHS).transpose(1, 0, 2, 3, 4).reshape(NG, G, RHS)
        rhs = excitation[step].astype(jnp.float32) - field
        solved = jnp.einsum('gab,gbr->gar', self_inverse, rhs, precision=lax.Precision.HIGHEST).astype(jnp.bfloat16)
        currents = currents.at[step].set(solved)
    return currents
```

```python
import functools

import jax
import jax.numpy as jnp
from jax import lax
from jax.experimental import pallas as pl
from jax.experimental.pallas import tpu as pltpu
from jax.sharding import PartitionSpec as P

LAGS = 8
STEPS = 4
SIDE = 4
ROWS = 16
COLS = 8
GROUP = 256
RHS = 128
OWN = 64
HELP = 24
CAP = 4
POOL = ROWS * CAP
MESH = pl.DeviceIdType.MESH
F32 = jnp.float32
BF16 = jnp.bfloat16
VMEM_LIMIT = 60 * 2**20


def history_kernel(
    own_obs, own_src, own_lag, aid_ok, aid_obs, aid_src, aid_lag,
    history, tiles, pool, out, past, own_buf, aid_buf, acc, sem_past, sem_own, sem_aid, sem_out,
):
    chunk = 8
    past_copies = [
        pltpu.make_async_copy(
            history.at[p], past.at[:, :, pl.ds(p * RHS, RHS)], sem_past.at[p]
        )
        for p in range(LAGS)
    ]
    own_copies = [
        pltpu.make_async_copy(
            tiles.at[pl.ds(i * chunk, chunk)], own_buf.at[pl.ds(i * chunk, chunk)], sem_own.at[i]
        )
        for i in range(OWN // chunk)
    ]
    aid_copies = [
        pltpu.make_async_copy(
            pool.at[pl.ds(i * chunk, chunk)], aid_buf.at[pl.ds(i * chunk, chunk)], sem_aid.at[i]
        )
        for i in range(POOL // chunk)
    ]
    for copy in past_copies + own_copies + aid_copies:
        copy.start()
    past[:, :, pl.ds(LAGS * RHS, 3 * RHS)] = jnp.zeros((COLS, GROUP, 3 * RHS), BF16)
    acc[...] = jnp.zeros(acc.shape, F32)
    for copy in past_copies:
        copy.wait()

    def add(tile, obs, src, lag):
        first = pl.multiple_of((LAGS - lag) * RHS, RHS)
        window = past[src, :, pl.ds(first, STEPS * RHS)]
        acc[obs] += jnp.dot(tile, window, preferred_element_type=F32)

    for i in range(OWN // chunk):
        own_copies[i].wait()

        @pl.loop(i * chunk, (i + 1) * chunk)
        def _(t):
            add(own_buf[t], own_obs[t], own_src[t], own_lag[t])

    for i in range(POOL // chunk):
        aid_copies[i].wait()

        @pl.loop(i * chunk, (i + 1) * chunk)
        def _(t):
            @pl.when(aid_ok[t] != 0)
            def _():
                add(aid_buf[t], aid_obs[t], aid_src[t], aid_lag[t])

    copy = pltpu.make_async_copy(acc, out, sem_out)
    copy.start()
    copy.wait()


def history_fields(own_meta, aid_meta, history, tiles, pool):
    smem = pl.BlockSpec(memory_space=pltpu.SMEM)
    hbm = pl.BlockSpec(memory_space=pl.ANY)
    return pl.pallas_call(
        history_kernel,
        out_shape=jax.ShapeDtypeStruct((ROWS, GROUP, STEPS * RHS), F32),
        in_specs=[smem] * 7 + [hbm] * 3,
        out_specs=hbm,
        scratch_shapes=[
            pltpu.VMEM((COLS, GROUP, (LAGS + 3) * RHS), BF16),
            pltpu.VMEM((OWN, GROUP, GROUP), BF16),
            pltpu.VMEM((POOL, GROUP, GROUP), BF16),
            pltpu.VMEM((ROWS, GROUP, STEPS * RHS), F32),
            pltpu.SemaphoreType.DMA((LAGS,)),
            pltpu.SemaphoreType.DMA((OWN // 8,)),
            pltpu.SemaphoreType.DMA((POOL // 8,)),
            pltpu.SemaphoreType.DMA,
        ],
        compiler_params=pltpu.CompilerParams(vmem_limit_bytes=VMEM_LIMIT),
    )(*own_meta, *aid_meta, history, tiles, pool)


def march_kernel(
    perm, index, keep, last, slab_hbm, tiles_hbm, inverse, excitation, out,
    slab, tiles, table, cur0, cur1, cur2, seg, mine,
    tx1, rx1, tx2, rx2,
    sem_slab, sem_tiles, s_tx1, s_rx1, s_tx2, s_rx2, s_ztx, s_zrx, s_ctx, s_crx,
):
    row = lax.axis_index("src")
    col = lax.axis_index("obs")
    y, x = row // SIDE, lax.rem(row, SIDE)
    z, core = col // 2, lax.rem(col, 2)
    half = GROUP // 2
    cur = [cur0, cur1, cur2]

    def turn(v, d):
        return lax.rem(v + d + SIDE, SIDE)

    def plane(yy, xx):
        return (yy * SIDE + xx, col)

    partners = (
        [plane(y, turn(x, d)) for d in (1, 2, 3)]
        + [plane(turn(y, d), x) for d in (1, 2, 3)]
        + [(row, turn(z, d) * 2 + core) for d in (1, 2, 3)]
        + [(row, z * 2 + 1 - core)]
    )
    slab_copy = pltpu.make_async_copy(slab_hbm, slab, sem_slab)
    tiles_copy = pltpu.make_async_copy(tiles_hbm, tiles, sem_tiles)
    slab_copy.start()
    tiles_copy.start()
    barrier = pltpu.get_barrier_semaphore()
    for device in partners:
        pl.semaphore_signal(barrier, inc=1, device_id=device, device_id_type=MESH)
    table[3 * COLS] = jnp.zeros((GROUP, RHS), BF16)
    seg[OWN] = jnp.zeros((GROUP, RHS), F32)
    slab_copy.wait()
    pl.semaphore_wait(barrier, len(partners))
    sent = []

    for step in range(STEPS):
        if step:

            def product(k, carry):
                term = jnp.dot(
                    tiles[perm[k]],
                    table[index[(step - 1) * OWN + k]],
                    preferred_element_type=F32,
                )
                total = carry * keep[k] + term
                seg[k] = total
                return total

            lax.fori_loop(0, OWN, product, jnp.zeros((GROUP, RHS), F32))

        def field(obs, part):
            value = slab[obs, pl.ds(part * half, half), pl.ds(step * RHS, RHS)]
            if step:
                value = value + seg[last[obs], pl.ds(part * half, half), :]
            return value

        def owner(part, other, along):
            return other * SIDE + along if part == 0 else along * SIDE + other

        def toward(part, along):
            return plane(y, along) if part == 0 else plane(along, x)

        here = (x, y)
        first = {}
        for d in (2, 1, 3):
            for part in (0, 1):
                along = turn(here[part], d)
                for other in range(SIDE):
                    tx1[step, part, d - 1, other] = field(
                        owner(part, other, along), part
                    ).astype(BF16)
                copy = pltpu.make_async_remote_copy(
                    src_ref=tx1.at[step, part, d - 1],
                    dst_ref=rx1.at[step, part, d - 1],
                    send_sem=s_tx1.at[step, part, d - 1],
                    recv_sem=s_rx1.at[step, part, d - 1],
                    device_id=toward(part, along),
                    device_id_type=MESH,
                )
                copy.start()
                first[part, d] = copy
                sent.append(copy)
        second = {}
        for part in (0, 1):
            for d in (1, 3, 2):
                first[part, d].wait_recv()

            def summed(other):
                value = field(owner(part, other, here[part]), part)
                for d in (1, 2, 3):
                    value = value + rx1[step, part, d - 1, other].astype(F32)
                return value

            for d in (2, 1, 3):
                other = turn(here[1 - part], d)
                tx2[step, part, d - 1] = summed(other)
                copy = pltpu.make_async_remote_copy(
                    src_ref=tx2.at[step, part, d - 1],
                    dst_ref=rx2.at[step, part, d - 1],
                    send_sem=s_tx2.at[step, part, d - 1],
                    recv_sem=s_rx2.at[step, part, d - 1],
                    device_id=toward(1 - part, other),
                    device_id_type=MESH,
                )
                copy.start()
                second[part, d] = copy
                sent.append(copy)
            mine[pl.ds(part * half, half), :] = summed(here[1 - part])
        for part in (0, 1):
            rows = pl.ds(part * half, half)
            value = mine[rows, :]
            for d in (1, 3, 2):
                second[part, d].wait_recv()
                value = value + rx2[step, part, d - 1]
            mine[rows, :] = excitation[step, 0, rows, :].astype(F32) - value
        solved = jnp.dot(
            inverse[0], mine[...], precision=lax.Precision.HIGHEST, preferred_element_type=F32
        ).astype(BF16)
        out[step, 0] = solved
        if step == STEPS - 1:
            break
        now = cur[step]
        now[col] = solved

        def along_z(e):
            return pltpu.make_async_remote_copy(
                src_ref=now.at[col],
                dst_ref=now.at[col],
                send_sem=s_ztx.at[step, e - 1],
                recv_sem=s_zrx.at[step, e - 1],
                device_id=(row, turn(z, e) * 2 + core),
                device_id_type=MESH,
            )

        def to_sibling(e):
            block = turn(z, -e) * 2 + core
            return pltpu.make_async_remote_copy(
                src_ref=now.at[block],
                dst_ref=now.at[block],
                send_sem=s_ctx.at[step, e],
                recv_sem=s_crx.at[step, e],
                device_id=(row, z * 2 + 1 - core),
                device_id_type=MESH,
            )

        spread = {e: along_z(e) for e in (1, 2, 3)}
        across = {e: to_sibling(e) for e in range(SIDE)}
        for e in (2, 1, 3):
            spread[e].start()
        across[0].start()
        for e in (1, 3, 2):
            spread[e].wait_recv()
            across[e].start()
        if step == 0:
            tiles_copy.wait()
        for e in (0, 1, 3, 2):
            across[e].wait_recv()
        table[pl.ds(step * COLS, COLS)] = now[...]
        sent += list(spread.values()) + list(across.values())
    for copy in sent:
        copy.wait_send()


def march(perm, index, keep, last, slab, tiles, inverse, excitation):
    smem = pl.BlockSpec(memory_space=pltpu.SMEM)
    hbm = pl.BlockSpec(memory_space=pl.ANY)
    vmem = pl.BlockSpec(memory_space=pltpu.VMEM)
    half = GROUP // 2
    dma = pltpu.SemaphoreType.DMA
    return pl.pallas_call(
        march_kernel,
        out_shape=jax.ShapeDtypeStruct((STEPS, 1, GROUP, RHS), BF16),
        in_specs=[smem] * 4 + [hbm] * 2 + [vmem] * 2,
        out_specs=vmem,
        scratch_shapes=[
            pltpu.VMEM((ROWS, GROUP, STEPS * RHS), F32),
            pltpu.VMEM((OWN, GROUP, GROUP), BF16),
            pltpu.VMEM((3 * COLS + 1, GROUP, RHS), BF16),
            pltpu.VMEM((COLS, GROUP, RHS), BF16),
            pltpu.VMEM((COLS, GROUP, RHS), BF16),
            pltpu.VMEM((COLS, GROUP, RHS), BF16),
            pltpu.VMEM((OWN + 1, GROUP, RHS), F32),
            pltpu.VMEM((GROUP, RHS), F32),
            pltpu.VMEM((STEPS, 2, 3, SIDE, half, RHS), BF16),
            pltpu.VMEM((STEPS, 2, 3, SIDE, half, RHS), BF16),
            pltpu.VMEM((STEPS, 2, 3, half, RHS), F32),
            pltpu.VMEM((STEPS, 2, 3, half, RHS), F32),
            dma,
            dma,
            dma((STEPS, 2, 3)),
            dma((STEPS, 2, 3)),
            dma((STEPS, 2, 3)),
            dma((STEPS, 2, 3)),
            dma((STEPS - 1, 3)),
            dma((STEPS - 1, 3)),
            dma((STEPS - 1, SIDE)),
            dma((STEPS - 1, SIDE)),
        ],
        compiler_params=pltpu.CompilerParams(
            collective_id=0, has_side_effects=True, vmem_limit_bytes=VMEM_LIMIT
        ),
    )(perm, index, keep, last, slab, tiles, inverse, excitation)


def sorted_tables(tile_obs, tile_src, tile_lag):
    place = jnp.arange(OWN, dtype=jnp.int32)
    key = tile_obs * OWN + place
    rank = jnp.sum((key[None, :] < key[:, None]).astype(jnp.int32), axis=1)
    pick = (rank[None, :] == place[:, None]).astype(jnp.int32)
    perm = jnp.sum(pick * place[None, :], axis=1)
    obs = jnp.sum(pick * tile_obs[None, :], axis=1)
    src = jnp.sum(pick * tile_src[None, :], axis=1)
    lag = jnp.sum(pick * tile_lag[None, :], axis=1)
    before = jnp.concatenate([jnp.full((1,), -1, jnp.int32), obs[:-1]])
    keep = (obs == before).astype(F32)
    steps = jnp.arange(1, STEPS, dtype=jnp.int32)[:, None]
    index = jnp.where(lag[None, :] <= steps, (steps - lag[None, :]) * COLS + src[None, :], 3 * COLS)
    slabs = jnp.arange(ROWS, dtype=jnp.int32)
    upto = jnp.sum((tile_obs[None, :] <= slabs[:, None]).astype(jnp.int32), axis=1)
    count = jnp.sum((tile_obs[None, :] == slabs[:, None]).astype(jnp.int32), axis=1)
    last = jnp.where(count > 0, upto - 1, OWN)
    return perm, index.reshape(-1), keep, last


def swap_help(help_tiles, help_obs, help_src, help_lag, row, column):
    src = lax.dynamic_index_in_dim(help_src.reshape(ROWS, COLS, HELP), column, 1, keepdims=False)
    lag = lax.dynamic_index_in_dim(help_lag.reshape(ROWS, COLS, HELP), column, 1, keepdims=False)
    target = src // COLS
    order = jnp.arange(HELP, dtype=jnp.int32)
    earlier = (target[:, :, None] == target[:, None, :]) & (order[None, None, :] < order[None, :, None])
    slot = jnp.sum(earlier.astype(jnp.int32), axis=2)
    mine_target = lax.dynamic_index_in_dim(target, row, 0, keepdims=False)
    mine_slot = lax.dynamic_index_in_dim(slot, row, 0, keepdims=False)
    place = jnp.arange(POOL, dtype=jnp.int32)
    sends = (mine_target * CAP + mine_slot)[None, :] == place[:, None]
    pick = jnp.sum(jnp.where(sends, order[None, :], 0), axis=1)
    tiles_out = jnp.take(help_tiles, pick, axis=0).reshape(ROWS, CAP, GROUP, GROUP)
    pool = lax.all_to_all(tiles_out, "src", split_axis=0, concat_axis=0, tiled=True)
    every_obs = lax.all_gather(help_obs, "src", axis=0, tiled=False)
    slots = jnp.arange(CAP, dtype=jnp.int32)
    got = (target[:, None, :] == row) & (slot[:, None, :] == slots[None, :, None])
    ok = jnp.any(got, axis=2).astype(jnp.int32).reshape(-1)

    def gathered(values):
        return jnp.sum(jnp.where(got, values[:, None, :], 0), axis=2).reshape(-1)

    aid_lag = jnp.where(ok != 0, gathered(lag), LAGS)
    meta = (ok, gathered(every_obs), gathered(src % COLS), aid_lag)
    return pool.reshape(POOL, GROUP, GROUP), meta


def on_device(
    history, tiles, tile_obs, tile_src, tile_lag,
    help_tiles, help_obs, help_src, help_lag, self_inverse, excitation,
):
    row = lax.axis_index("src")
    column = lax.axis_index("obs")
    pool, aid_meta = swap_help(help_tiles, help_obs, help_src, help_lag, row, column)
    slab = history_fields((tile_obs, tile_src, tile_lag), aid_meta, history, tiles, pool)
    perm, index, keep, last = sorted_tables(tile_obs, tile_src, tile_lag)
    return march(perm, index, keep, last, slab, tiles, self_inverse, excitation)


def solution(mesh):
    placed = (
        P(None, "src", None, None),
        P(("src", "obs"), None, None),
        P(("src", "obs")),
        P(("src", "obs")),
        P(("src", "obs")),
        P(("src", "obs"), None, None),
        P(("src", "obs")),
        P(),
        P(),
        P(("src", "obs"), None, None),
        P(None, ("src", "obs"), None, None),
    )
    return jax.shard_map(
        on_device,
        mesh=mesh,
        in_specs=placed,
        out_specs=P(None, ("src", "obs"), None, None),
        check_vma=False,
    )
```

```python
import functools

import jax
import jax.numpy as jnp
from jax import lax
from jax.experimental import pallas as pl
from jax.experimental.pallas import tpu as pltpu
from jax.sharding import PartitionSpec as P

LAGS = 8
STEPS = 4
SIDE = 4
ROWS = 16
COLS = 8
GROUP = 256
RHS = 128
OWN = 64
HELP = 24
CAP = 4
POOL = ROWS * CAP
ROUNDS = 22
CHOICES = (19, 20, 22)
SLOTS = HELP + 8 + 4 * ROUNDS
MESH = pl.DeviceIdType.MESH
F32 = jnp.float32
BF16 = jnp.bfloat16
VMEM_LIMIT = 60 * 2**20


def plan_kernel(src, lag, moves, final, rounds, state):
    lane = lax.broadcasted_iota(jnp.int32, (HELP, ROWS * COLS), 1)
    tile = lax.broadcasted_iota(jnp.int32, (HELP, ROWS * COLS), 0)
    row = lane // COLS
    target = src[...] // COLS
    left_x = (target % SIDE - row % SIDE) & 3
    left_y = (target // SIDE - row // SIDE) & 3
    state[pl.ds(0, HELP)] = (
        left_x | (left_y << 2) | (((row << 5) | tile) << 4)
        | ((src[...] % COLS) << 13) | ((lag[...] - 3) << 16)
    )
    state[pl.ds(HELP, SLOTS - HELP)] = jnp.zeros((SLOTS - HELP, ROWS * COLS), jnp.int32)
    slot = lax.broadcasted_iota(jnp.int32, (SLOTS, ROWS * COLS), 0)
    one = lax.broadcasted_iota(jnp.int32, (1, ROWS * COLS), 1)
    x_here = (one // COLS) % SIDE

    def link(number, now):
        along, up = number < 2, number % 2 == 0
        left = now & 3 if along else (now >> 2) & 3
        rest = (now >> 2) & 3 if along else now & 3
        may = (left == (1 if up else 3)) | (left == 2)
        hops = jnp.where(left == 3, 1, left) + jnp.where(rest == 3, 1, rest)
        rank = hops * 4 + jnp.where(rest == 0, 2, 0) + jnp.where(left == 2, 0, 1)
        key = jnp.where(may, (rank << 26) | (slot << 19) | now, 0)
        best = jnp.max(key, axis=0, keepdims=True)
        now = jnp.where(may & (key == best), 0, now)
        record = best & ((1 << 19) - 1)
        step = -1 if up else 1
        if along:
            record = (record & ~3) | ((record + step) & 3)
        else:
            record = (record & ~12) | ((record + 4 * step) & 12)
        record = jnp.where(best > 0, record, 0)
        if along:
            near = pltpu.roll(record, COLS if up else ROWS * COLS - COLS, 1)
            wrap = pltpu.roll(record, ROWS * COLS - 3 * COLS if up else 3 * COLS, 1)
            record = jnp.where(x_here == (0 if up else SIDE - 1), wrap, near)
        else:
            shift = SIDE * COLS
            record = pltpu.roll(record, shift if up else ROWS * COLS - shift, 1)
        return now, record, jnp.where(best > 0, (best >> 19) & 127, 0), best > 0

    def one_round(t, order, carry):
        used, older, old = carry
        for i in range(4):
            state[pl.ds(HELP + 4 * t + i, 1)] = older[i]
        now = state[...]
        fresh = [None] * 4
        for number in order:
            now, fresh[number], pick, moved = link(number, now)
            moves[pl.ds(4 * t + number, 1)] = pick
            used = jnp.where(moved, t + 1, used)
        state[...] = now
        return used, old, tuple(fresh)

    def two_rounds(i, carry):
        carry = one_round(2 * i, (0, 1, 2, 3), carry)
        return one_round(2 * i + 1, (2, 3, 0, 1), carry)

    empty = jnp.zeros((1, ROWS * COLS), jnp.int32)
    none = (empty,) * 4
    used, older, old = lax.fori_loop(0, ROUNDS // 2, two_rounds, (empty, none, none))
    for i in range(4):
        state[pl.ds(HELP + 4 * ROUNDS + i, 1)] = older[i]
        state[pl.ds(HELP + 4 * ROUNDS + 4 + i, 1)] = old[i]
    now = state[...]
    final[...] = now[HELP + 8 :]
    rounds[0] = jnp.max(used) + ROUNDS * jnp.max(jnp.where((now & 15) != 0, 1, 0))


def plan_routes(src, lag):
    vmem = pl.BlockSpec(memory_space=pltpu.VMEM)
    shape = jax.ShapeDtypeStruct((4 * ROUNDS, ROWS * COLS), jnp.int32)
    return pl.pallas_call(
        plan_kernel,
        out_shape=(shape, shape, jax.ShapeDtypeStruct((1,), jnp.int32)),
        in_specs=[vmem] * 2,
        out_specs=(vmem, vmem, pl.BlockSpec(memory_space=pltpu.SMEM)),
        scratch_shapes=[pltpu.VMEM((SLOTS, ROWS * COLS), jnp.int32)],
    )(src, lag)


def route_kernel(
    rounds, moves, help_tiles, help_obs, out, every_obs,
    pool, landed, stage, obs_in, sem_in, sem_out, s_tx, s_rx, s_otx, s_orx,
):
    row = lax.axis_index("src")
    col = lax.axis_index("obs")
    y, x = row // SIDE, lax.rem(row, SIDE)

    def at(dy, dx):
        return (lax.rem(y + dy, SIDE) * SIDE + lax.rem(x + dx, SIDE), col)

    others = [(dy, dx) for dy in range(SIDE) for dx in range(SIDE) if (dy, dx) != (0, 0)]
    links = [at(0, 1), at(0, SIDE - 1), at(1, 0), at(SIDE - 1, 0)]
    fetch = pltpu.make_async_copy(help_tiles, pool.at[pl.ds(0, HELP)], sem_in)
    fetch.start()
    barrier = pltpu.get_barrier_semaphore()
    for dy, dx in others:
        pl.semaphore_signal(barrier, inc=1, device_id=at(dy, dx), device_id_type=MESH)
    pool[pl.ds(HELP, 8)] = jnp.zeros((8, GROUP, GROUP), BF16)
    obs_in[row] = help_obs[...]
    fetch.wait()
    pl.semaphore_wait(barrier, len(others))
    notes = []
    for i, (dy, dx) in enumerate(others):
        note = pltpu.make_async_remote_copy(
            src_ref=help_obs,
            dst_ref=obs_in.at[row],
            send_sem=s_otx.at[i],
            recv_sem=s_orx.at[i],
            device_id=at(dy, dx),
            device_id_type=MESH,
        )
        note.start()
        notes.append(note)

    def hop(t, number):
        place = lax.rem(t, 2) * 4 + number
        return pltpu.make_async_remote_copy(
            src_ref=stage.at[place],
            dst_ref=landed.at[4 * t + number],
            send_sem=s_tx.at[place],
            recv_sem=s_rx.at[4 * t + number],
            device_id=links[number],
            device_id_type=MESH,
        )

    def keep(t, number):
        return pltpu.make_async_copy(
            landed.at[4 * t + number], out.at[4 * t + number], sem_out.at[4 * t + number]
        )

    def send(t):
        for number in range(4):
            stage[lax.rem(t, 2) * 4 + number] = pool[moves[4 * t + number]]
            hop(t, number).start()

    def take(t):
        for number in range(4):
            hop(t, number).wait_recv()
            keep(t, number).start()

    send(0)
    send(1)

    @pl.loop(2, rounds)
    def _(t):
        take(t - 2)
        for number in range(4):
            pool[HELP + 8 + 4 * (t - 2) + number] = landed[4 * (t - 2) + number]
            hop(t - 2, number).wait_send()
        send(t)

    for t in (rounds - 2, rounds - 1):
        take(t)
        for number in range(4):
            hop(t, number).wait_send()
    for note in notes:
        note.wait()
    every_obs[...] = obs_in[...]

    @pl.loop(0, rounds)
    def _(t):
        for number in range(4):
            keep(t, number).wait()


def route(rounds, collective, moves, help_tiles, help_obs):
    vmem = pl.BlockSpec(memory_space=pltpu.VMEM)
    hbm = pl.BlockSpec(memory_space=pl.ANY)
    dma = pltpu.SemaphoreType.DMA
    return pl.pallas_call(
        functools.partial(route_kernel, rounds),
        out_shape=(
            jax.ShapeDtypeStruct((4 * ROUNDS, GROUP, GROUP), BF16),
            jax.ShapeDtypeStruct((ROWS, 8, 128), jnp.int32),
        ),
        in_specs=[pl.BlockSpec(memory_space=pltpu.SMEM), hbm, vmem],
        out_specs=(hbm, vmem),
        scratch_shapes=[
            pltpu.VMEM((HELP + 8 + 4 * rounds, GROUP, GROUP), BF16),
            pltpu.VMEM((4 * rounds, GROUP, GROUP), BF16),
            pltpu.VMEM((8, GROUP, GROUP), BF16),
            pltpu.VMEM((ROWS, 8, 128), jnp.int32),
            dma,
            dma((4 * rounds,)),
            dma((8,)),
            dma((4 * rounds,)),
            dma((ROWS - 1,)),
            dma((ROWS - 1,)),
        ],
        compiler_params=pltpu.CompilerParams(
            collective_id=collective, has_side_effects=True, vmem_limit_bytes=VMEM_LIMIT
        ),
    )(moves, help_tiles, help_obs)


def history_kernel(
    own_obs, own_src, own_lag, aid, aid_obs,
    history, tiles, pool, out, past, own_buf, aid_buf, acc, sem_past, sem_own, sem_aid, sem_out,
):
    chunk = 8
    past_copies = [
        pltpu.make_async_copy(
            history.at[p], past.at[:, :, pl.ds(p * RHS, RHS)], sem_past.at[p]
        )
        for p in range(LAGS)
    ]
    own_copies = [
        pltpu.make_async_copy(
            tiles.at[pl.ds(i * chunk, chunk)], own_buf.at[pl.ds(i * chunk, chunk)], sem_own.at[i]
        )
        for i in range(OWN // chunk)
    ]
    for copy in past_copies + own_copies:
        copy.start()

    def arrived(t):
        return (aid[t] != 0) & ((aid[t] & 15) == 0)

    def aid_copy(t):
        return pltpu.make_async_copy(pool.at[t], aid_buf.at[t], sem_aid.at[t])

    @pl.loop(0, 4 * ROUNDS)
    def _(t):
        @pl.when(arrived(t))
        def _():
            aid_copy(t).start()

    past[:, :, pl.ds(LAGS * RHS, 3 * RHS)] = jnp.zeros((COLS, GROUP, 3 * RHS), BF16)
    acc[...] = jnp.zeros(acc.shape, F32)
    for copy in past_copies:
        copy.wait()

    def add(tile, obs, src, lag):
        first = pl.multiple_of((LAGS - lag) * RHS, RHS)
        window = past[src, :, pl.ds(first, STEPS * RHS)]
        acc[obs] += jnp.dot(tile, window, preferred_element_type=F32)

    for i in range(OWN // chunk):
        own_copies[i].wait()

        @pl.loop(i * chunk, (i + 1) * chunk)
        def _(t):
            add(own_buf[t], own_obs[t], own_src[t], own_lag[t])

    @pl.loop(0, 4 * ROUNDS)
    def _(t):
        @pl.when(arrived(t))
        def _():
            note = aid[t]
            aid_copy(t).wait()
            obs = aid_obs[(note >> 9) & 15, (note >> 4) & 31]
            add(aid_buf[t], obs, (note >> 13) & 7, ((note >> 16) & 7) + 3)

    copy = pltpu.make_async_copy(acc, out, sem_out)
    copy.start()
    copy.wait()


def history_fields(own_meta, aid, aid_obs, history, tiles, pool):
    smem = pl.BlockSpec(memory_space=pltpu.SMEM)
    hbm = pl.BlockSpec(memory_space=pl.ANY)
    return pl.pallas_call(
        history_kernel,
        out_shape=jax.ShapeDtypeStruct((ROWS, GROUP, STEPS * RHS), F32),
        in_specs=[smem] * 5 + [hbm] * 3,
        out_specs=hbm,
        scratch_shapes=[
            pltpu.VMEM((COLS, GROUP, (LAGS + 3) * RHS), BF16),
            pltpu.VMEM((OWN, GROUP, GROUP), BF16),
            pltpu.VMEM((4 * ROUNDS, GROUP, GROUP), BF16),
            pltpu.VMEM((ROWS, GROUP, STEPS * RHS), F32),
            pltpu.SemaphoreType.DMA((LAGS,)),
            pltpu.SemaphoreType.DMA((OWN // 8,)),
            pltpu.SemaphoreType.DMA((4 * ROUNDS,)),
            pltpu.SemaphoreType.DMA,
        ],
        compiler_params=pltpu.CompilerParams(vmem_limit_bytes=VMEM_LIMIT),
    )(*own_meta, aid, aid_obs, history, tiles, pool)


def march_kernel(
    perm, index, keep, last, slab_hbm, tiles_hbm, inverse, excitation, out,
    slab, tiles, table, cur0, cur1, cur2, seg, mine,
    tx1, rx1, tx2, rx2,
    sem_slab, sem_tiles, s_tx1, s_rx1, s_tx2, s_rx2, s_ztx, s_zrx, s_ctx, s_crx,
):
    row = lax.axis_index("src")
    col = lax.axis_index("obs")
    y, x = row // SIDE, lax.rem(row, SIDE)
    z, core = col // 2, lax.rem(col, 2)
    half = GROUP // 2
    cur = [cur0, cur1, cur2]

    def turn(v, d):
        return lax.rem(v + d + SIDE, SIDE)

    def plane(yy, xx):
        return (yy * SIDE + xx, col)

    partners = (
        [plane(y, turn(x, d)) for d in (1, 2, 3)]
        + [plane(turn(y, d), x) for d in (1, 2, 3)]
        + [(row, turn(z, d) * 2 + core) for d in (1, 2, 3)]
        + [(row, z * 2 + 1 - core)]
    )
    slab_copy = pltpu.make_async_copy(slab_hbm, slab, sem_slab)
    tiles_copy = pltpu.make_async_copy(tiles_hbm, tiles, sem_tiles)
    slab_copy.start()
    tiles_copy.start()
    barrier = pltpu.get_barrier_semaphore()
    for device in partners:
        pl.semaphore_signal(barrier, inc=1, device_id=device, device_id_type=MESH)
    table[3 * COLS] = jnp.zeros((GROUP, RHS), BF16)
    seg[OWN] = jnp.zeros((GROUP, RHS), F32)
    slab_copy.wait()
    pl.semaphore_wait(barrier, len(partners))
    sent = []

    for step in range(STEPS):
        if step:

            def product(k, carry):
                term = jnp.dot(
                    tiles[perm[k]],
                    table[index[(step - 1) * OWN + k]],
                    preferred_element_type=F32,
                )
                total = carry * keep[k] + term
                seg[k] = total
                return total

            lax.fori_loop(0, OWN, product, jnp.zeros((GROUP, RHS), F32))

        def field(obs, part):
            value = slab[obs, pl.ds(part * half, half), pl.ds(step * RHS, RHS)]
            if step:
                value = value + seg[last[obs], pl.ds(part * half, half), :]
            return value

        def owner(part, other, along):
            return other * SIDE + along if part == 0 else along * SIDE + other

        def toward(part, along):
            return plane(y, along) if part == 0 else plane(along, x)

        here = (x, y)
        first = {}
        for d in (2, 1, 3):
            for part in (0, 1):
                along = turn(here[part], d)
                for other in range(SIDE):
                    tx1[step, part, d - 1, other] = field(
                        owner(part, other, along), part
                    ).astype(BF16)
                copy = pltpu.make_async_remote_copy(
                    src_ref=tx1.at[step, part, d - 1],
                    dst_ref=rx1.at[step, part, d - 1],
                    send_sem=s_tx1.at[step, part, d - 1],
                    recv_sem=s_rx1.at[step, part, d - 1],
                    device_id=toward(part, along),
                    device_id_type=MESH,
                )
                copy.start()
                first[part, d] = copy
                sent.append(copy)
        second = {}
        for part in (0, 1):
            for d in (1, 3, 2):
                first[part, d].wait_recv()

            def summed(other):
                value = field(owner(part, other, here[part]), part)
                for d in (1, 2, 3):
                    value = value + rx1[step, part, d - 1, other].astype(F32)
                return value

            for d in (2, 1, 3):
                other = turn(here[1 - part], d)
                tx2[step, part, d - 1] = summed(other)
                copy = pltpu.make_async_remote_copy(
                    src_ref=tx2.at[step, part, d - 1],
                    dst_ref=rx2.at[step, part, d - 1],
                    send_sem=s_tx2.at[step, part, d - 1],
                    recv_sem=s_rx2.at[step, part, d - 1],
                    device_id=toward(1 - part, other),
                    device_id_type=MESH,
                )
                copy.start()
                second[part, d] = copy
                sent.append(copy)
            mine[pl.ds(part * half, half), :] = summed(here[1 - part])
        for part in (0, 1):
            rows = pl.ds(part * half, half)
            value = mine[rows, :]
            for d in (1, 3, 2):
                second[part, d].wait_recv()
                value = value + rx2[step, part, d - 1]
            mine[rows, :] = excitation[step, 0, rows, :].astype(F32) - value
        solved = jnp.dot(
            inverse[0], mine[...], precision=lax.Precision.HIGHEST, preferred_element_type=F32
        ).astype(BF16)
        out[step, 0] = solved
        if step == STEPS - 1:
            break
        now = cur[step]
        now[col] = solved

        def along_z(e):
            return pltpu.make_async_remote_copy(
                src_ref=now.at[col],
                dst_ref=now.at[col],
                send_sem=s_ztx.at[step, e - 1],
                recv_sem=s_zrx.at[step, e - 1],
                device_id=(row, turn(z, e) * 2 + core),
                device_id_type=MESH,
            )

        def to_sibling(e):
            block = turn(z, -e) * 2 + core
            return pltpu.make_async_remote_copy(
                src_ref=now.at[block],
                dst_ref=now.at[block],
                send_sem=s_ctx.at[step, e],
                recv_sem=s_crx.at[step, e],
                device_id=(row, z * 2 + 1 - core),
                device_id_type=MESH,
            )

        spread = {e: along_z(e) for e in (1, 2, 3)}
        across = {e: to_sibling(e) for e in range(SIDE)}
        for e in (2, 1, 3):
            spread[e].start()
        across[0].start()
        for e in (1, 3, 2):
            spread[e].wait_recv()
            across[e].start()
        if step == 0:
            tiles_copy.wait()
        for e in (0, 1, 3, 2):
            across[e].wait_recv()
        table[pl.ds(step * COLS, COLS)] = now[...]
        sent += list(spread.values()) + list(across.values())
    for copy in sent:
        copy.wait_send()


def march(perm, index, keep, last, slab, tiles, inverse, excitation):
    smem = pl.BlockSpec(memory_space=pltpu.SMEM)
    hbm = pl.BlockSpec(memory_space=pl.ANY)
    vmem = pl.BlockSpec(memory_space=pltpu.VMEM)
    half = GROUP // 2
    dma = pltpu.SemaphoreType.DMA
    return pl.pallas_call(
        march_kernel,
        out_shape=jax.ShapeDtypeStruct((STEPS, 1, GROUP, RHS), BF16),
        in_specs=[smem] * 4 + [hbm] * 2 + [vmem] * 2,
        out_specs=vmem,
        scratch_shapes=[
            pltpu.VMEM((ROWS, GROUP, STEPS * RHS), F32),
            pltpu.VMEM((OWN, GROUP, GROUP), BF16),
            pltpu.VMEM((3 * COLS + 1, GROUP, RHS), BF16),
            pltpu.VMEM((COLS, GROUP, RHS), BF16),
            pltpu.VMEM((COLS, GROUP, RHS), BF16),
            pltpu.VMEM((COLS, GROUP, RHS), BF16),
            pltpu.VMEM((OWN + 1, GROUP, RHS), F32),
            pltpu.VMEM((GROUP, RHS), F32),
            pltpu.VMEM((STEPS, 2, 3, SIDE, half, RHS), BF16),
            pltpu.VMEM((STEPS, 2, 3, SIDE, half, RHS), BF16),
            pltpu.VMEM((STEPS, 2, 3, half, RHS), F32),
            pltpu.VMEM((STEPS, 2, 3, half, RHS), F32),
            dma,
            dma,
            dma((STEPS, 2, 3)),
            dma((STEPS, 2, 3)),
            dma((STEPS, 2, 3)),
            dma((STEPS, 2, 3)),
            dma((STEPS - 1, 3)),
            dma((STEPS - 1, 3)),
            dma((STEPS - 1, SIDE)),
            dma((STEPS - 1, SIDE)),
        ],
        compiler_params=pltpu.CompilerParams(
            collective_id=0, has_side_effects=True, vmem_limit_bytes=VMEM_LIMIT
        ),
    )(perm, index, keep, last, slab, tiles, inverse, excitation)


def sorted_tables(tile_obs, tile_src, tile_lag):
    place = jnp.arange(OWN, dtype=jnp.int32)
    key = tile_obs * OWN + place
    rank = jnp.sum((key[None, :] < key[:, None]).astype(jnp.int32), axis=1)
    pick = (rank[None, :] == place[:, None]).astype(jnp.int32)
    perm = jnp.sum(pick * place[None, :], axis=1)
    obs = jnp.sum(pick * tile_obs[None, :], axis=1)
    src = jnp.sum(pick * tile_src[None, :], axis=1)
    lag = jnp.sum(pick * tile_lag[None, :], axis=1)
    before = jnp.concatenate([jnp.full((1,), -1, jnp.int32), obs[:-1]])
    keep = (obs == before).astype(F32)
    steps = jnp.arange(1, STEPS, dtype=jnp.int32)[:, None]
    index = jnp.where(lag[None, :] <= steps, (steps - lag[None, :]) * COLS + src[None, :], 3 * COLS)
    slabs = jnp.arange(ROWS, dtype=jnp.int32)
    upto = jnp.sum((tile_obs[None, :] <= slabs[:, None]).astype(jnp.int32), axis=1)
    count = jnp.sum((tile_obs[None, :] == slabs[:, None]).astype(jnp.int32), axis=1)
    last = jnp.where(count > 0, upto - 1, OWN)
    return perm, index.reshape(-1), keep, last


def swap_help(help_tiles, help_obs, help_src, help_lag, row, column):
    src = lax.dynamic_index_in_dim(help_src.reshape(ROWS, COLS, HELP), column, 1, keepdims=False)
    lag = lax.dynamic_index_in_dim(help_lag.reshape(ROWS, COLS, HELP), column, 1, keepdims=False)
    target = src // COLS
    order = jnp.arange(HELP, dtype=jnp.int32)
    earlier = (target[:, :, None] == target[:, None, :]) & (order[None, None, :] < order[None, :, None])
    slot = jnp.sum(earlier.astype(jnp.int32), axis=2)
    mine_target = lax.dynamic_index_in_dim(target, row, 0, keepdims=False)
    mine_slot = lax.dynamic_index_in_dim(slot, row, 0, keepdims=False)
    place = jnp.arange(POOL, dtype=jnp.int32)
    sends = (mine_target * CAP + mine_slot)[None, :] == place[:, None]
    pick = jnp.sum(jnp.where(sends, order[None, :], 0), axis=1)
    tiles_out = jnp.take(help_tiles, pick, axis=0).reshape(ROWS, CAP, GROUP, GROUP)
    pool = lax.all_to_all(tiles_out, "src", split_axis=0, concat_axis=0, tiled=True)
    every_obs = lax.all_gather(help_obs, "src", axis=0, tiled=False)
    slots = jnp.arange(CAP, dtype=jnp.int32)
    got = (target[:, None, :] == row) & (slot[:, None, :] == slots[None, :, None])
    rows = jnp.arange(ROWS, dtype=jnp.int32)
    note = (((rows[:, None] << 5) | order[None, :]) << 4) | ((src % COLS) << 13) | ((lag - 3) << 16)
    aid = jnp.sum(jnp.where(got, note[:, None, :], 0), axis=2).reshape(-1)
    spare = 4 * ROUNDS - POOL
    pool = jnp.pad(pool.reshape(POOL, GROUP, GROUP), ((0, spare), (0, 0), (0, 0)))
    return pool, jnp.pad(every_obs, ((0, 0), (0, 128 - HELP))), jnp.pad(aid, (0, spare))


def on_device(
    history, tiles, tile_obs, tile_src, tile_lag,
    help_tiles, help_obs, help_src, help_lag, self_inverse, excitation,
):
    row = lax.axis_index("src")
    column = lax.axis_index("obs")
    moves, final, rounds = plan_routes(
        help_src.reshape(ROWS * COLS, HELP).T, help_lag.reshape(ROWS * COLS, HELP).T
    )
    lane = row * COLS + column
    own_moves = lax.dynamic_index_in_dim(moves, lane, 1, keepdims=False)
    own_final = lax.dynamic_index_in_dim(final, lane, 1, keepdims=False)

    def routed(count, collective):
        def run():
            own_obs = jnp.zeros((8, 128), jnp.int32).at[0, :HELP].set(help_obs)
            pool, every_obs = route(count, collective, own_moves, help_tiles, own_obs)
            return pool, every_obs[:, 0, :], own_final

        return run

    def general():
        return swap_help(help_tiles, help_obs, help_src, help_lag, row, column)

    branches = [routed(count, 1 + i) for i, count in enumerate(CHOICES)] + [general]
    choice = sum((rounds[0] > count).astype(jnp.int32) for count in CHOICES)
    pool, every_obs, aid = lax.switch(choice, branches)
    slab = history_fields((tile_obs, tile_src, tile_lag), aid, every_obs, history, tiles, pool)
    perm, index, keep, last = sorted_tables(tile_obs, tile_src, tile_lag)
    return march(perm, index, keep, last, slab, tiles, self_inverse, excitation)


def solution(mesh):
    placed = (
        P(None, "src", None, None),
        P(("src", "obs"), None, None),
        P(("src", "obs")),
        P(("src", "obs")),
        P(("src", "obs")),
        P(("src", "obs"), None, None),
        P(("src", "obs")),
        P(),
        P(),
        P(("src", "obs"), None, None),
        P(None, ("src", "obs"), None, None),
    )
    return jax.shard_map(
        on_device,
        mesh=mesh,
        in_specs=placed,
        out_specs=P(None, ("src", "obs"), None, None),
        check_vma=False,
    )
```

```python
import functools

import jax
import jax.numpy as jnp
from jax import lax
from jax.experimental import pallas as pl
from jax.experimental.pallas import tpu as pltpu
from jax.sharding import PartitionSpec as P

LAGS = 8
STEPS = 4
SIDE = 4
ROWS = 16
COLS = 8
GROUP = 256
RHS = 128
OWN = 64
HELP = 24
CAP = 4
POOL = ROWS * CAP
ROUNDS = 22
MIDDLE = 8
LIST1, LIST23, EVERY = 0, 7, 14
SLOTS1, SLOTS23 = 20, 32
CHOICES = (19, 20, 22)
SLOTS = HELP + 8 + 4 * ROUNDS
MESH = pl.DeviceIdType.MESH
F32 = jnp.float32
BF16 = jnp.bfloat16
VMEM_LIMIT = 60 * 2**20


def plan_kernel(requests, moves, final, rounds, state):
    lane = lax.broadcasted_iota(jnp.int32, (HELP, ROWS * COLS), 1)
    tile = lax.broadcasted_iota(jnp.int32, (HELP, ROWS * COLS), 0)
    row = lane // COLS
    src, lag = requests[...] & 255, requests[...] >> 8
    target = src // COLS
    left_x = (target % SIDE - row % SIDE) & 3
    left_y = (target // SIDE - row // SIDE) & 3
    state[pl.ds(0, HELP)] = (
        left_x | (left_y << 2) | (((row << 5) | tile) << 4)
        | ((src % COLS) << 13) | ((lag - 3) << 16)
    )
    state[pl.ds(HELP, SLOTS - HELP)] = jnp.zeros((SLOTS - HELP, ROWS * COLS), jnp.int32)
    slot = lax.broadcasted_iota(jnp.int32, (SLOTS, ROWS * COLS), 0)
    one = lax.broadcasted_iota(jnp.int32, (1, ROWS * COLS), 1)
    x_here = (one // COLS) % SIDE

    def link(number, now):
        along, up = number < 2, number % 2 == 0
        left = now & 3 if along else (now >> 2) & 3
        rest = (now >> 2) & 3 if along else now & 3
        may = (left == (1 if up else 3)) | (left == 2)
        hops = jnp.where(left == 3, 1, left) + jnp.where(rest == 3, 1, rest)
        rank = hops * 4 + jnp.where(rest == 0, 2, 0) + jnp.where(left == 2, 0, 1)
        key = jnp.where(may, (rank << 26) | (slot << 19) | now, 0)
        best = jnp.max(key, axis=0, keepdims=True)
        now = jnp.where(may & (key == best), 0, now)
        record = best & ((1 << 19) - 1)
        step = -1 if up else 1
        if along:
            record = (record & ~3) | ((record + step) & 3)
        else:
            record = (record & ~12) | ((record + 4 * step) & 12)
        record = jnp.where(best > 0, record, 0)
        if along:
            near = pltpu.roll(record, COLS if up else ROWS * COLS - COLS, 1)
            wrap = pltpu.roll(record, ROWS * COLS - 3 * COLS if up else 3 * COLS, 1)
            record = jnp.where(x_here == (0 if up else SIDE - 1), wrap, near)
        else:
            shift = SIDE * COLS
            record = pltpu.roll(record, shift if up else ROWS * COLS - shift, 1)
        return now, record, jnp.where(best > 0, (best >> 19) & 127, 0), best > 0

    def one_round(t, order, carry):
        used, older, old = carry
        for i in range(4):
            state[pl.ds(HELP + 4 * t + i, 1)] = older[i]
        now = state[...]
        fresh = [None] * 4
        for number in order:
            now, fresh[number], pick, moved = link(number, now)
            moves[pl.ds(4 * t + number, 1)] = pick
            used = jnp.where(moved, t + 1, used)
        state[...] = now
        return used, old, tuple(fresh)

    def two_rounds(i, carry):
        carry = one_round(2 * i, (0, 1, 2, 3), carry)
        return one_round(2 * i + 1, (2, 3, 0, 1), carry)

    empty = jnp.zeros((1, ROWS * COLS), jnp.int32)
    none = (empty,) * 4
    used, older, old = lax.fori_loop(0, ROUNDS // 2, two_rounds, (empty, none, none))
    for i in range(4):
        state[pl.ds(HELP + 4 * ROUNDS + i, 1)] = older[i]
        state[pl.ds(HELP + 4 * ROUNDS + 4 + i, 1)] = old[i]
    now = state[...]
    final[...] = now[HELP + 8 :]
    rounds[0] = jnp.max(used) + ROUNDS * jnp.max(jnp.where((now & 15) != 0, 1, 0))


def plan_routes(requests):
    vmem = pl.BlockSpec(memory_space=pltpu.VMEM)
    shape = jax.ShapeDtypeStruct((4 * ROUNDS, ROWS * COLS), jnp.int32)
    return pl.pallas_call(
        plan_kernel,
        out_shape=(shape, shape, jax.ShapeDtypeStruct((1,), jnp.int32)),
        in_specs=[vmem],
        out_specs=(vmem, vmem, pl.BlockSpec(memory_space=pltpu.SMEM)),
        scratch_shapes=[pltpu.VMEM((SLOTS, ROWS * COLS), jnp.int32)],
    )(requests)


def history_copies(history, past, sems):
    return [
        pltpu.make_async_copy(history.at[p], past.at[:, :, pl.ds(p * RHS, RHS)], sems.at[p])
        for p in range(LAGS)
    ]


def route_kernel(
    rounds, moves, tables, help_tiles, history, tiles, notice, out, sums, every_obs, most,
    pool, landed, stage, notices, peak, peaks, past, own_buf, seg,
    sem_in, sem_out, s_tx, s_rx, s_otx, s_orx, s_ptx, s_prx, sem_past, sem_own, sem_seg,
):
    row = lax.axis_index("src")
    col = lax.axis_index("obs")
    y, x = row // SIDE, lax.rem(row, SIDE)

    def at(dy, dx):
        return (lax.rem(y + dy, SIDE) * SIDE + lax.rem(x + dx, SIDE), col)

    others = [(dy, dx) for dy in range(SIDE) for dx in range(SIDE) if (dy, dx) != (0, 0)]
    links = [at(0, 1), at(0, SIDE - 1), at(1, 0), at(SIDE - 1, 0)]
    fetch = pltpu.make_async_copy(help_tiles, pool.at[pl.ds(0, HELP)], sem_in)
    fetch.start()
    past_copy = pltpu.make_async_copy(history, past.at[pl.ds(0, LAGS * COLS)], sem_past)
    own_copy = pltpu.make_async_copy(tiles, own_buf, sem_own)
    past_copy.start()
    own_copy.start()
    barrier = pltpu.get_barrier_semaphore()
    for dy, dx in others:
        pl.semaphore_signal(barrier, inc=1, device_id=at(dy, dx), device_id_type=MESH)
    columns = [(row, lax.rem(col + d, COLS)) for d in range(1, COLS)]
    for device in columns:
        pl.semaphore_signal(barrier, inc=1, device_id=device, device_id_type=MESH)
    pool[pl.ds(HELP, 8)] = jnp.zeros((8, GROUP, GROUP), BF16)
    notices[row] = notice[...]
    fetch.wait()
    pl.semaphore_wait(barrier, len(others) + len(columns))
    notes = []
    for i, (dy, dx) in enumerate(others):
        note = pltpu.make_async_remote_copy(
            src_ref=notice,
            dst_ref=notices.at[row],
            send_sem=s_otx.at[i],
            recv_sem=s_orx.at[i],
            device_id=at(dy, dx),
            device_id_type=MESH,
        )
        note.start()
        notes.append(note)

    def hop(t, number):
        place = lax.rem(t, 2) * 4 + number
        return pltpu.make_async_remote_copy(
            src_ref=stage.at[place],
            dst_ref=landed.at[4 * t + number],
            send_sem=s_tx.at[place],
            recv_sem=s_rx.at[4 * t + number],
            device_id=links[number],
            device_id_type=MESH,
        )

    def keep(t, number):
        return pltpu.make_async_copy(
            landed.at[4 * t + number], out.at[4 * t + number], sem_out.at[4 * t + number]
        )

    def send(t):
        for number in range(4):
            stage[lax.rem(t, 2) * 4 + number] = pool[moves[4 * t + number]]
            hop(t, number).start()

    def take(t):
        for number in range(4):
            hop(t, number).wait_recv()
            keep(t, number).start()

    send(0)
    send(1)

    def save(k, place):
        return pltpu.make_async_copy(seg.at[place], sums.at[k], sem_seg.at[place])

    def own_fields(t):
        for i in range(4):
            k = 4 * (t - 2) + i

            @pl.when(t > 2)
            def _():
                save(k - 4, i).wait()

            first = tables[EVERY + 6, k]
            window = jnp.concatenate([past[first + p * COLS] for p in range(STEPS)], axis=1)
            term = jnp.dot(own_buf[tables[EVERY, k]], window, preferred_element_type=F32)
            seg[i] = seg[(i + 3) % 4] * tables[EVERY + 1, k].astype(F32) + term
            save(k, i).start()

    def advance(t):
        take(t - 2)
        for number in range(4):
            pool[HELP + 8 + 4 * (t - 2) + number] = landed[4 * (t - 2) + number]
            hop(t - 2, number).wait_send()
        send(t)

    def both(t):
        advance(t)
        own_fields(t)

    past[pl.ds(LAGS * COLS, 3 * COLS)] = jnp.zeros((3 * COLS, GROUP, RHS), BF16)
    seg[3] = jnp.zeros((GROUP, STEPS * RHS), F32)
    past_copy.wait()
    own_copy.wait()
    pl.loop(2, MIDDLE)(both)
    for note in notes:
        note.wait()
    every_obs[...] = notices[...]
    peak[...] = jnp.max(notices[...], axis=0)
    peaks[col] = peak[...]
    tops = []
    for i, device in enumerate(columns):
        top = pltpu.make_async_remote_copy(
            src_ref=peak,
            dst_ref=peaks.at[col],
            send_sem=s_ptx.at[i],
            recv_sem=s_prx.at[i],
            device_id=device,
            device_id_type=MESH,
        )
        top.start()
        tops.append(top)
    pl.loop(MIDDLE, OWN // 4 + 2)(both)
    pl.loop(OWN // 4 + 2, rounds)(advance)
    for i in range(4):
        save(OWN - 4 + i, i).wait()
    for t in (rounds - 2, rounds - 1):
        take(t)
        for number in range(4):
            hop(t, number).wait_send()
    for top in tops:
        top.wait()
    most[...] = jnp.max(peaks[...], axis=0)

    @pl.loop(0, rounds)
    def _(t):
        for number in range(4):
            keep(t, number).wait()


def route(rounds, collective, moves, tables, help_tiles, history, tiles, notice):
    vmem = pl.BlockSpec(memory_space=pltpu.VMEM)
    hbm = pl.BlockSpec(memory_space=pl.ANY)
    dma = pltpu.SemaphoreType.DMA
    return pl.pallas_call(
        functools.partial(route_kernel, rounds),
        out_shape=(
            jax.ShapeDtypeStruct((4 * ROUNDS, GROUP, GROUP), BF16),
            jax.ShapeDtypeStruct((OWN, GROUP, STEPS * RHS), F32),
            jax.ShapeDtypeStruct((ROWS, 8, 128), jnp.int32),
            jax.ShapeDtypeStruct((8, 128), jnp.int32),
        ),
        in_specs=[pl.BlockSpec(memory_space=pltpu.SMEM)] * 2 + [hbm] * 3 + [vmem],
        out_specs=(hbm, hbm, vmem, vmem),
        scratch_shapes=[
            pltpu.VMEM((HELP + 8 + 4 * rounds, GROUP, GROUP), BF16),
            pltpu.VMEM((4 * rounds, GROUP, GROUP), BF16),
            pltpu.VMEM((8, GROUP, GROUP), BF16),
            pltpu.VMEM((ROWS, 8, 128), jnp.int32),
            pltpu.VMEM((8, 128), jnp.int32),
            pltpu.VMEM((COLS, 8, 128), jnp.int32),
            pltpu.VMEM(((LAGS + 3) * COLS, GROUP, RHS), BF16),
            pltpu.VMEM((OWN, GROUP, GROUP), BF16),
            pltpu.VMEM((4, GROUP, STEPS * RHS), F32),
            dma,
            dma((4 * rounds,)),
            dma((8,)),
            dma((4 * rounds,)),
            dma((ROWS - 1,)),
            dma((ROWS - 1,)),
            dma((COLS - 1,)),
            dma((COLS - 1,)),
            dma,
            dma,
            dma((4,)),
        ],
        compiler_params=pltpu.CompilerParams(
            collective_id=collective, has_side_effects=True, vmem_limit_bytes=VMEM_LIMIT
        ),
    )(moves, tables, help_tiles, history, tiles, notice)


def history_kernel(
    aid, aid_obs, tables, history, sums, pool, out,
    listed, past, aid_buf, acc, sem_past, sem_aid, sem_acc, sem_out,
):
    past_copies = history_copies(history, past, sem_past)
    for copy in past_copies:
        copy.start()
    empty = 4 * ROUNDS

    def aid_copy(t):
        return pltpu.make_async_copy(pool.at[t], aid_buf.at[t], sem_aid.at[t])

    def gather(t, count):
        here = (aid[t] != 0) & ((aid[t] & 15) == 0)

        @pl.when(here)
        def _():
            aid_copy(t).start()

        listed[count] = t
        return count + here.astype(jnp.int32)

    def acc_copy(obs):
        return pltpu.make_async_copy(
            sums.at[tables[EVERY + 5, obs] - 1], acc.at[obs], sem_acc.at[obs]
        )

    @pl.loop(0, ROWS)
    def _(obs):
        @pl.when(tables[EVERY + 5, obs] > 0)
        def _():
            acc_copy(obs).start()

        @pl.when(tables[EVERY + 5, obs] == 0)
        def _():
            acc[obs] = jnp.zeros((GROUP, STEPS * RHS), F32)

    count = lax.fori_loop(0, 4 * ROUNDS, gather, 0)
    for i in range(4):
        listed[count + i] = empty
    aid_buf[empty] = jnp.zeros((GROUP, GROUP), BF16)
    past[:, :, pl.ds(LAGS * RHS, 3 * RHS)] = jnp.zeros((COLS, GROUP, 3 * RHS), BF16)
    for copy in past_copies:
        copy.wait()

    @pl.loop(0, count)
    def _(i):
        aid_copy(listed[i]).wait()

    @pl.loop(0, ROWS)
    def _(obs):
        @pl.when(tables[EVERY + 5, obs] > 0)
        def _():
            acc_copy(obs).wait()

    @pl.loop(0, (count + 3) // 4)
    def _(group):
        for i in range(4):
            t = listed[4 * group + i]
            live = t < empty
            note = jnp.where(live, aid[jnp.minimum(t, empty - 1)], 5 << 16)
            obs = aid_obs[(note >> 9) & 15, (note >> 4) & 31]
            lag = ((note >> 16) & 7) + 3
            first = pl.multiple_of((LAGS - lag) * RHS, RHS)
            window = past[(note >> 13) & 7, :, pl.ds(first, STEPS * RHS)]
            acc[obs] += jnp.dot(aid_buf[t], window, preferred_element_type=F32)

    copy = pltpu.make_async_copy(acc, out, sem_out)
    copy.start()
    copy.wait()


def history_fields(aid, aid_obs, tables, history, sums, pool):
    smem = pl.BlockSpec(memory_space=pltpu.SMEM)
    hbm = pl.BlockSpec(memory_space=pl.ANY)
    return pl.pallas_call(
        history_kernel,
        out_shape=jax.ShapeDtypeStruct((ROWS, GROUP, STEPS * RHS), F32),
        in_specs=[smem] * 3 + [hbm] * 3,
        out_specs=hbm,
        scratch_shapes=[
            pltpu.SMEM((4 * ROUNDS + 8,), jnp.int32),
            pltpu.VMEM((COLS, GROUP, (LAGS + 3) * RHS), BF16),
            pltpu.VMEM((4 * ROUNDS + 1, GROUP, GROUP), BF16),
            pltpu.VMEM((ROWS, GROUP, STEPS * RHS), F32),
            pltpu.SemaphoreType.DMA((LAGS,)),
            pltpu.SemaphoreType.DMA((4 * ROUNDS,)),
            pltpu.SemaphoreType.DMA((ROWS,)),
            pltpu.SemaphoreType.DMA,
        ],
        compiler_params=pltpu.CompilerParams(vmem_limit_bytes=VMEM_LIMIT),
    )(aid, aid_obs, tables, history, sums, pool)


def march_kernel(
    slots1, slots23, tables, slab_hbm, tiles_hbm, inverse, excitation, out,
    slab, tiles, table, cur00, cur01, cur10, cur11, cur20, cur21, seg1, seg23, own, mine, right,
    tx1, rx1, tx2, rx2,
    sem_slab, sem_tiles, s_tx1, s_rx1, s_tx2, s_rx2, s_ztx, s_zrx, s_ctx, s_crx,
):
    row = lax.axis_index("src")
    col = lax.axis_index("obs")
    y, x = row // SIDE, lax.rem(row, SIDE)
    z, core = col // 2, lax.rem(col, 2)
    half, quarter = GROUP // 2, GROUP // 4
    cur = [[cur00, cur01], [cur10, cur11], [cur20, cur21]]
    lane = lax.broadcasted_iota(jnp.int32, (1, RHS), 1)
    in_half = [lane < RHS // 2, lane >= RHS // 2]
    here = (x, y)

    def turn(v, d):
        return lax.rem(v + d + SIDE, SIDE)

    def swap(value):
        return pltpu.roll(value, RHS // 2, 1)

    def plane(yy, xx):
        return (yy * SIDE + xx, col)

    partners = (
        [plane(y, turn(x, d)) for d in (1, 2, 3)]
        + [plane(turn(y, d), x) for d in (1, 2, 3)]
        + [(row, turn(z, d) * 2 + core) for d in (1, 2, 3)]
        + [(row, z * 2 + 1 - core)]
    )
    slab_copy = pltpu.make_async_copy(slab_hbm, slab, sem_slab)
    tiles_copy = pltpu.make_async_copy(tiles_hbm, tiles, sem_tiles)
    slab_copy.start()
    tiles_copy.start()
    barrier = pltpu.get_barrier_semaphore()
    for device in partners:
        pl.semaphore_signal(barrier, inc=1, device_id=device, device_id_type=MESH)
    table[...] = jnp.zeros(table.shape, BF16)
    seg1[0] = jnp.zeros((GROUP, RHS), F32)
    seg23[0] = jnp.zeros((GROUP, RHS), F32)
    slab_copy.wait()
    pl.semaphore_wait(barrier, len(partners))
    sent = []
    first, second, spread, across = {}, {}, {}, {}

    def products(seg, base, step, begin, end):
        def product(k, carry):
            term = jnp.dot(
                tiles[tables[base, k]],
                table[tables[base + 1 + step, k]],
                preferred_element_type=F32,
            )
            total = carry * tables[base + 1, k].astype(F32) + term
            seg[k + 1] = total
            return total

        lax.fori_loop(begin, end, product, seg[begin], unroll=4)

    def owner(part, other, along):
        return other * SIDE + along if part == 0 else along * SIDE + other

    def toward(part, along):
        return plane(y, along) if part == 0 else plane(along, x)

    def piece(step, part, obs):
        rows = pl.ds(part * half, half)
        value = slab[obs, rows, pl.ds(step * RHS, RHS)]
        if step >= 1:
            value = value + seg1[tables[LIST1 + 5, obs], rows, :]
        if step >= 2:
            value = value + seg23[tables[LIST23 + 5, obs], rows, :]
        return value

    def packed(step, h, part, along, pair):
        even = piece(step, part, owner(part, 2 * pair, along))
        odd = piece(step, part, owner(part, 2 * pair + 1, along))
        return jnp.where(in_half[h], even, swap(odd))

    def send_first(step, h):
        for d in (2, 1, 3):
            for part in (0, 1):
                along = turn(here[part], d)
                for pair in (0, 1):
                    tx1[step, h, part, d - 1, pair] = packed(step, h, part, along, pair).astype(BF16)
                copy = pltpu.make_async_remote_copy(
                    src_ref=tx1.at[step, h, part, d - 1],
                    dst_ref=rx1.at[step, h, part, d - 1],
                    send_sem=s_tx1.at[step, h, part, d - 1],
                    recv_sem=s_rx1.at[step, h, part, d - 1],
                    device_id=toward(part, along),
                    device_id_type=MESH,
                )
                copy.start()
                first[step, h, part, d] = copy
                sent.append(copy)
        for part in (0, 1):
            for pair in (0, 1):
                own[h, part, pair] = packed(step, h, part, here[part], pair)

    def send_second(step, h):
        for part in (0, 1):
            for d in (1, 3, 2):
                first[step, h, part, d].wait_recv()
            for pair in (0, 1):
                value = own[h, part, pair]
                for d in (1, 2, 3):
                    value = value + rx1[step, h, part, d - 1, pair].astype(F32)
                own[h, part, pair] = value

            def block(other):
                value = own[h, part, other // 2]
                value = jnp.where(lax.rem(other, 2) == 1, swap(value), value)
                return jnp.where(in_half[h], value[:quarter], swap(value[quarter:]))

            for d in (2, 1, 3):
                other = turn(here[1 - part], d)
                tx2[step, h, part, d - 1] = block(other)
                copy = pltpu.make_async_remote_copy(
                    src_ref=tx2.at[step, h, part, d - 1],
                    dst_ref=rx2.at[step, h, part, d - 1],
                    send_sem=s_tx2.at[step, h, part, d - 1],
                    recv_sem=s_rx2.at[step, h, part, d - 1],
                    device_id=toward(1 - part, other),
                    device_id_type=MESH,
                )
                copy.start()
                second[step, h, part, d] = copy
                sent.append(copy)
            mine[h, part] = block(here[1 - part])

    def solve(step, h):
        for part in (0, 1):
            value = mine[h, part]
            for d in (1, 3, 2):
                second[step, h, part, d].wait_recv()
                value = value + rx2[step, h, part, d - 1]
            for i, rows_value in enumerate((value, swap(value))):
                rows = pl.ds(part * half + i * quarter, quarter)
                right[rows, :] = excitation[step, 0, rows, :].astype(F32) - rows_value
        solved = jnp.dot(
            inverse[0], right[...], precision=lax.Precision.HIGHEST, preferred_element_type=F32
        )
        if step < STEPS - 1:
            now = cur[step][h]
            now[col] = jnp.where(in_half[h], solved[:half], swap(solved[half:])).astype(BF16)
            for e in (2, 1, 3):
                spread[step, h, e] = pltpu.make_async_remote_copy(
                    src_ref=now.at[col],
                    dst_ref=now.at[col],
                    send_sem=s_ztx.at[step, h, e - 1],
                    recv_sem=s_zrx.at[step, h, e - 1],
                    device_id=(row, turn(z, e) * 2 + core),
                    device_id_type=MESH,
                )
                spread[step, h, e].start()
                sent.append(spread[step, h, e])
            to_sibling(step, h, 0)
        if h == 0:
            out[step, 0] = solved.astype(BF16)
        else:
            out[step, 0] = jnp.where(in_half[h], solved, out[step, 0].astype(F32)).astype(BF16)

    def to_sibling(step, h, e):
        now = cur[step][h]
        block = turn(z, -e) * 2 + core
        across[step, h, e] = pltpu.make_async_remote_copy(
            src_ref=now.at[block],
            dst_ref=now.at[block],
            send_sem=s_ctx.at[step, h, e],
            recv_sem=s_crx.at[step, h, e],
            device_id=(row, z * 2 + 1 - core),
            device_id_type=MESH,
        )
        across[step, h, e].start()
        sent.append(across[step, h, e])

    def forward(step, h):
        for e in (1, 3, 2):
            spread[step, h, e].wait_recv()
            to_sibling(step, h, e)

    def collect(step, h):
        for e in (0, 1, 3, 2):
            across[step, h, e].wait_recv()

        @pl.loop(0, COLS)
        def _(g):
            value = cur[step][h][g].astype(F32)
            for i, part in enumerate((value, swap(value))):
                rows = pl.ds(i * half, half)
                if h == 1:
                    part = jnp.where(in_half[h], part, table[step * COLS + g, rows, :].astype(F32))
                table[step * COLS + g, rows, :] = part.astype(BF16)

    for step in range(STEPS):
        for h in (0, 1):
            if step:
                forward(step - 1, h)
                collect(step - 1, h)
                if step == 1 and h == 0:
                    tiles_copy.wait()
                products(seg1, LIST1, step, 0, slots1)
            send_first(step, h)
        early = 1 <= step < STEPS - 1
        if early:
            products(seg23, LIST23, step + 1, 0, slots23 // 2)
        for h in (0, 1):
            send_second(step, h)
        if early:
            products(seg23, LIST23, step + 1, slots23 // 2, slots23)
        for h in (0, 1):
            solve(step, h)
    for copy in sent:
        copy.wait_send()


def march(slots1, slots23, collective, tables, slab, tiles, inverse, excitation):
    hbm = pl.BlockSpec(memory_space=pl.ANY)
    vmem = pl.BlockSpec(memory_space=pltpu.VMEM)
    half = GROUP // 2
    dma = pltpu.SemaphoreType.DMA
    return pl.pallas_call(
        functools.partial(march_kernel, slots1, slots23),
        out_shape=jax.ShapeDtypeStruct((STEPS, 1, GROUP, RHS), BF16),
        in_specs=[pl.BlockSpec(memory_space=pltpu.SMEM)] + [hbm] * 2 + [vmem] * 2,
        out_specs=vmem,
        scratch_shapes=[
            pltpu.VMEM((ROWS, GROUP, STEPS * RHS), F32),
            pltpu.VMEM((OWN, GROUP, GROUP), BF16),
            pltpu.VMEM((3 * COLS + 1, GROUP, RHS), BF16),
        ]
        + [pltpu.VMEM((COLS, half, RHS), BF16)] * 6
        + [
            pltpu.VMEM((slots1 + 1, GROUP, RHS), F32),
            pltpu.VMEM((slots23 + 1, GROUP, RHS), F32),
            pltpu.VMEM((2, 2, 2, half, RHS), F32),
            pltpu.VMEM((2, 2, half // 2, RHS), F32),
            pltpu.VMEM((GROUP, RHS), F32),
            pltpu.VMEM((STEPS, 2, 2, 3, 2, half, RHS), BF16),
            pltpu.VMEM((STEPS, 2, 2, 3, 2, half, RHS), BF16),
            pltpu.VMEM((STEPS, 2, 2, 3, half // 2, RHS), F32),
            pltpu.VMEM((STEPS, 2, 2, 3, half // 2, RHS), F32),
            dma,
            dma,
            dma((STEPS, 2, 2, 3)),
            dma((STEPS, 2, 2, 3)),
            dma((STEPS, 2, 2, 3)),
            dma((STEPS, 2, 2, 3)),
            dma((STEPS - 1, 2, 3)),
            dma((STEPS - 1, 2, 3)),
            dma((STEPS - 1, 2, SIDE)),
            dma((STEPS - 1, 2, SIDE)),
        ],
        compiler_params=pltpu.CompilerParams(
            collective_id=collective, has_side_effects=True, vmem_limit_bytes=VMEM_LIMIT
        ),
    )(tables, slab, tiles, inverse, excitation)


def sorted_list(member, tile_obs, tile_src, tile_lag):
    place = jnp.arange(OWN, dtype=jnp.int32)
    key = jnp.where(member, tile_obs, ROWS) * OWN + place
    rank = jnp.sum((key[None, :] < key[:, None]).astype(jnp.int32), axis=1)
    pick = rank[None, :] == place[:, None]
    steps = jnp.arange(1, STEPS, dtype=jnp.int32)[:, None]
    live = member[None, :] & (tile_lag[None, :] <= steps)
    use = jnp.where(live, (steps - tile_lag[None, :]) * COLS + tile_src[None, :], 3 * COLS)
    same = (tile_obs[None, :] == tile_obs[:, None]) & member[None, :] & member[:, None]
    joined = jnp.any(same & (place[None, :] < place[:, None]), axis=1).astype(jnp.int32)
    columns = jnp.concatenate(
        [place[None], joined[None], use, (LAGS - tile_lag[None]) * COLS + tile_src[None]], axis=0
    )
    values = jnp.sum(jnp.where(pick[None], columns[:, None, :], 0), axis=2)
    slabs = place[:, None]
    upto = jnp.sum((member[None, :] & (tile_obs[None, :] <= slabs)).astype(jnp.int32), axis=1)
    some = jnp.any(member[None, :] & (tile_obs[None, :] == slabs), axis=1)
    return jnp.concatenate([values[:5], jnp.where(some, upto, 0)[None], values[5:]], axis=0)


def swap_help(help_tiles, help_obs, help_src, help_lag, row, column):
    src = lax.dynamic_index_in_dim(help_src.reshape(ROWS, COLS, HELP), column, 1, keepdims=False)
    lag = lax.dynamic_index_in_dim(help_lag.reshape(ROWS, COLS, HELP), column, 1, keepdims=False)
    target = src // COLS
    order = jnp.arange(HELP, dtype=jnp.int32)
    earlier = (target[:, :, None] == target[:, None, :]) & (order[None, None, :] < order[None, :, None])
    slot = jnp.sum(earlier.astype(jnp.int32), axis=2)
    mine_target = lax.dynamic_index_in_dim(target, row, 0, keepdims=False)
    mine_slot = lax.dynamic_index_in_dim(slot, row, 0, keepdims=False)
    place = jnp.arange(POOL, dtype=jnp.int32)
    sends = (mine_target * CAP + mine_slot)[None, :] == place[:, None]
    pick = jnp.sum(jnp.where(sends, order[None, :], 0), axis=1)
    tiles_out = jnp.take(help_tiles, pick, axis=0).reshape(ROWS, CAP, GROUP, GROUP)
    pool = lax.all_to_all(tiles_out, "src", split_axis=0, concat_axis=0, tiled=True)
    every_obs = lax.all_gather(help_obs, "src", axis=0, tiled=False)
    slots = jnp.arange(CAP, dtype=jnp.int32)
    got = (target[:, None, :] == row) & (slot[:, None, :] == slots[None, :, None])
    rows = jnp.arange(ROWS, dtype=jnp.int32)
    note = (((rows[:, None] << 5) | order[None, :]) << 4) | ((src % COLS) << 13) | ((lag - 3) << 16)
    aid = jnp.sum(jnp.where(got, note[:, None, :], 0), axis=2).reshape(-1)
    spare = 4 * ROUNDS - POOL
    pool = jnp.pad(pool.reshape(POOL, GROUP, GROUP), ((0, spare), (0, 0), (0, 0)))
    return pool, jnp.pad(every_obs, ((0, 0), (0, 128 - HELP))), jnp.pad(aid, (0, spare))


def on_device(
    history, tiles, tile_obs, tile_src, tile_lag,
    help_tiles, help_obs, help_src, help_lag, self_inverse, excitation,
):
    row = lax.axis_index("src")
    column = lax.axis_index("obs")
    moves, final, rounds = plan_routes(
        (help_src | (help_lag << 8)).reshape(ROWS * COLS, HELP).T
    )
    lane = row * COLS + column
    own_moves = lax.dynamic_index_in_dim(moves, lane, 1, keepdims=False)
    own_final = lax.dynamic_index_in_dim(final, lane, 1, keepdims=False)

    flat_history = history.reshape(LAGS * COLS, GROUP, RHS)
    member1 = tile_lag == 1
    member23 = (tile_lag == 2) | (tile_lag == 3)
    counts = jnp.stack([jnp.sum(m.astype(jnp.int32)) for m in (member1, member23)])

    tables = jnp.concatenate(
        [
            sorted_list(member1, tile_obs, tile_src, tile_lag),
            sorted_list(member23, tile_obs, tile_src, tile_lag),
            sorted_list(tile_lag > 0, tile_obs, tile_src, tile_lag),
        ]
    )

    def routed(count, collective):
        def run():
            notice = jnp.concatenate(
                [
                    jnp.pad(help_obs, (0, 128 - HELP))[None],
                    jnp.broadcast_to(counts[:, None], (2, 128)),
                    jnp.zeros((5, 128), jnp.int32),
                ]
            )
            pool, sums, every, most = route(
                count, collective, own_moves, tables, help_tiles, flat_history, tiles, notice
            )
            return pool, sums, every[:, 0, :], own_final, most[1:3, 0]

        return run

    def general():
        most = lax.pmax(counts, ("src", "obs"))
        table = jnp.concatenate([history, jnp.zeros((3,) + history.shape[1:], BF16)])

        def add(total, entry):
            tile, joined, first = entry
            window = lax.dynamic_slice(
                table, (first // COLS, first % COLS, 0, 0), (STEPS, 1, GROUP, RHS)
            )[:, 0]
            term = jnp.einsum("ab,pbr->apr", tiles[tile], window, preferred_element_type=F32)
            total = jnp.where(joined != 0, total, 0.0) + term.reshape(GROUP, STEPS * RHS)
            return total, total

        entries = tuple(tables[EVERY + i] for i in (0, 1, 6))
        sums = lax.scan(add, jnp.zeros((GROUP, STEPS * RHS), F32), entries)[1]
        pool, every, aid = swap_help(help_tiles, help_obs, help_src, help_lag, row, column)
        return pool, sums, every, aid, most

    branches = [routed(count, 2 + i) for i, count in enumerate(CHOICES)] + [general]
    choice = sum((rounds[0] > count).astype(jnp.int32) for count in CHOICES)
    pool, sums, every_obs, aid, most = lax.switch(choice, branches)
    slab = history_fields(aid, every_obs, tables, history, sums, pool)

    def marched(slots1, slots23, collective):
        return lambda: march(
            slots1, slots23, collective, tables, slab, tiles, self_inverse, excitation
        )

    few = (most[0] <= SLOTS1) & (most[1] <= SLOTS23)
    return lax.cond(few, marched(SLOTS1, SLOTS23, 0), marched(OWN, OWN, 1))


def solution(mesh):
    placed = (
        P(None, "src", None, None),
        P(("src", "obs"), None, None),
        P(("src", "obs")),
        P(("src", "obs")),
        P(("src", "obs")),
        P(("src", "obs"), None, None),
        P(("src", "obs")),
        P(),
        P(),
        P(("src", "obs"), None, None),
        P(None, ("src", "obs"), None, None),
    )
    return jax.shard_map(
        on_device,
        mesh=mesh,
        in_specs=placed,
        out_specs=P(None, ("src", "obs"), None, None),
        check_vma=False,
    )
```

```python
import functools

import jax
import jax.numpy as jnp
from jax import lax
from jax.experimental import pallas as pl
from jax.experimental.pallas import tpu as pltpu
from jax.sharding import PartitionSpec as P

LAGS = 8
STEPS = 4
SIDE = 4
ROWS = 16
COLS = 8
GROUP = 256
RHS = 128
OWN = 64
HELP = 24
CAP = 4
POOL = ROWS * CAP
ROUNDS = 22
MIDDLE = 8
LIST1, LIST23, EVERY = 0, 7, 14
SLOTS1, SLOTS23 = 20, 32
CHOICES = (19, 20, 22)
SLOTS = HELP + 8 + 4 * ROUNDS
MESH = pl.DeviceIdType.MESH
F32 = jnp.float32
BF16 = jnp.bfloat16
VMEM_LIMIT = 60 * 2**20


def sorted_list(member, across, down):
    obs_r, obs_c, src_c, lag_c = across[0], down[0], down[1], down[2]
    in_r, in_c = member(across[2]).astype(jnp.int32), member(lag_c).astype(jnp.int32)
    place_r = lax.broadcasted_iota(jnp.int32, (1, OWN), 1)
    place_c = lax.broadcasted_iota(jnp.int32, (OWN, 1), 0)
    key_r = jnp.where(in_r > 0, obs_r, ROWS) * OWN + place_r
    key_c = jnp.where(in_c > 0, obs_c, ROWS) * OWN + place_c
    rank = jnp.sum(jnp.where(key_r < key_c, 1.0, 0.0), axis=1, keepdims=True).astype(jnp.int32)
    pick = rank == place_r
    same = jnp.where((obs_r == obs_c) & (place_r < place_c), in_r * in_c, 0)
    joined = jnp.max(same, axis=1, keepdims=True)

    def use(step):
        block = (step - lag_c) * COLS + src_c
        return jnp.where((in_c > 0) & (lag_c <= step), block, 3 * COLS)

    def placed(column):
        value = jnp.where(pick, column.astype(F32), 0.0)
        return jnp.sum(value, axis=0, keepdims=True).astype(jnp.int32)

    counted = in_c.astype(F32)
    upto = jnp.sum(jnp.where(obs_c <= place_r, counted, 0.0), axis=0, keepdims=True)
    some = jnp.sum(jnp.where(obs_c == place_r, counted, 0.0), axis=0, keepdims=True)
    last = jnp.where(some > 0, upto, 0.0).astype(jnp.int32)
    rows = [placed(place_c), placed(joined)] + [placed(use(step)) for step in (1, 2, 3)]
    rows += [last, placed((LAGS - lag_c) * COLS + src_c)]
    return rows, jnp.sum(counted, axis=0, keepdims=True).astype(jnp.int32)


def plan_kernel(requests, own_r, own_c, own_aid, moves, final, tables, notice, rounds, state):
    across = [own_r[pl.ds(i, 1), :] for i in range(3)]
    down = [own_c[:, pl.ds(i, 1)] for i in range(3)]
    members = (lambda lag: lag == 1, lambda lag: (lag == 2) | (lag == 3), lambda lag: lag > 0)
    notice[...] = jnp.zeros(notice.shape, jnp.int32)
    notice[pl.ds(0, 1), pl.ds(0, HELP)] = own_aid[...]
    for base, member in zip((LIST1, LIST23, EVERY), members):
        rows, count = sorted_list(member, across, down)
        for i, values in enumerate(rows):
            tables[pl.ds(base + i, 1), :] = values
        if base != EVERY:
            notice[pl.ds(1 + base // LIST23, 1), :] = jnp.broadcast_to(count, (1, 128))
    lane = lax.broadcasted_iota(jnp.int32, (HELP, ROWS * COLS), 1)
    tile = lax.broadcasted_iota(jnp.int32, (HELP, ROWS * COLS), 0)
    row = lane // COLS
    src, lag = requests[...] & 255, requests[...] >> 8
    target = src // COLS
    left_x = (target % SIDE - row % SIDE) & 3
    left_y = (target // SIDE - row // SIDE) & 3
    state[pl.ds(0, HELP)] = (
        left_x | (left_y << 2) | (((row << 5) | tile) << 4)
        | ((src % COLS) << 13) | ((lag - 3) << 16)
    )
    state[pl.ds(HELP, SLOTS - HELP)] = jnp.zeros((SLOTS - HELP, ROWS * COLS), jnp.int32)
    one = lax.broadcasted_iota(jnp.int32, (1, ROWS * COLS), 1)
    x_here = (one // COLS) % SIDE

    def link(number, now):
        along, up = number < 2, number % 2 == 0
        left = now & 3 if along else (now >> 2) & 3
        rest = (now >> 2) & 3 if along else now & 3
        may = (left == (1 if up else 3)) | (left == 2)
        slot = lax.broadcasted_iota(jnp.int32, now.shape, 0)
        hops = jnp.where(left == 3, 1, left) + jnp.where(rest == 3, 1, rest)
        rank = hops * 4 + jnp.where(rest == 0, 2, 0) + jnp.where(left == 2, 0, 1)
        key = jnp.where(may, (rank << 26) | (slot << 19) | now, 0)
        best = jnp.max(key, axis=0, keepdims=True)
        now = jnp.where(may & (key == best), 0, now)
        record = best & ((1 << 19) - 1)
        step = -1 if up else 1
        if along:
            record = (record & ~3) | ((record + step) & 3)
        else:
            record = (record & ~12) | ((record + 4 * step) & 12)
        record = jnp.where(best > 0, record, 0)
        if along:
            near = pltpu.roll(record, COLS if up else ROWS * COLS - COLS, 1)
            wrap = pltpu.roll(record, ROWS * COLS - 3 * COLS if up else 3 * COLS, 1)
            record = jnp.where(x_here == (0 if up else SIDE - 1), wrap, near)
        else:
            shift = SIDE * COLS
            record = pltpu.roll(record, shift if up else ROWS * COLS - shift, 1)
        return now, record, jnp.where(best > 0, (best >> 19) & 127, 0), best > 0

    def one_round(t, order, rows, carry):
        used, older, old = carry
        for i in range(4):
            state[pl.ds(HELP + 4 * t + i, 1)] = older[i]
        now = state[pl.ds(0, rows)]
        fresh = [None] * 4
        for number in order:
            now, fresh[number], pick, moved = link(number, now)
            moves[pl.ds(4 * t + number, 1)] = pick
            used = jnp.where(moved, t + 1, used)
        state[pl.ds(0, rows)] = now
        return used, old, tuple(fresh)

    def two_rounds(rows):
        def run(i, carry):
            carry = one_round(2 * i, (0, 1, 2, 3), rows, carry)
            return one_round(2 * i + 1, (2, 3, 0, 1), rows, carry)

        return run

    empty = jnp.zeros((1, ROWS * COLS), jnp.int32)
    none = (empty,) * 4
    carry = lax.fori_loop(0, 5, two_rounds(HELP + 40), (empty, none, none))
    used, older, old = lax.fori_loop(5, ROUNDS // 2, two_rounds(SLOTS), carry)
    for i in range(4):
        state[pl.ds(HELP + 4 * ROUNDS + i, 1)] = older[i]
        state[pl.ds(HELP + 4 * ROUNDS + 4 + i, 1)] = old[i]
    now = state[...]
    final[...] = now[HELP + 8 :]
    rounds[0] = jnp.max(used) + ROUNDS * jnp.max(jnp.where((now & 15) != 0, 1, 0))


def plan_routes(requests, own_r, own_c, own_aid):
    vmem = pl.BlockSpec(memory_space=pltpu.VMEM)
    shape = jax.ShapeDtypeStruct((4 * ROUNDS, ROWS * COLS), jnp.int32)
    return pl.pallas_call(
        plan_kernel,
        out_shape=(
            shape,
            shape,
            jax.ShapeDtypeStruct((3 * LIST23, OWN), jnp.int32),
            jax.ShapeDtypeStruct((8, 128), jnp.int32),
            jax.ShapeDtypeStruct((1,), jnp.int32),
        ),
        in_specs=[vmem] * 4,
        out_specs=(vmem,) * 4 + (pl.BlockSpec(memory_space=pltpu.SMEM),),
        scratch_shapes=[pltpu.VMEM((SLOTS, ROWS * COLS), jnp.int32)],
    )(requests, own_r, own_c, own_aid)


def history_copies(history, past, sems):
    return [
        pltpu.make_async_copy(history.at[p], past.at[:, :, pl.ds(p * RHS, RHS)], sems.at[p])
        for p in range(LAGS)
    ]


def route_kernel(
    rounds, moves, tables, help_tiles, history, tiles, notice, out, sums, every_obs, most,
    pool, landed, stage, notices, peak, peaks, past, own_buf, seg,
    sem_in, sem_out, s_tx, s_rx, s_otx, s_orx, s_ptx, s_prx, sem_past, sem_own, sem_seg,
):
    row = lax.axis_index("src")
    col = lax.axis_index("obs")
    y, x = row // SIDE, lax.rem(row, SIDE)

    def at(dy, dx):
        return (lax.rem(y + dy, SIDE) * SIDE + lax.rem(x + dx, SIDE), col)

    others = [(dy, dx) for dy in range(SIDE) for dx in range(SIDE) if (dy, dx) != (0, 0)]
    links = [at(0, 1), at(0, SIDE - 1), at(1, 0), at(SIDE - 1, 0)]
    fetch = pltpu.make_async_copy(help_tiles, pool.at[pl.ds(0, HELP)], sem_in)
    fetch.start()
    past_copy = pltpu.make_async_copy(history, past.at[pl.ds(0, LAGS * COLS)], sem_past)
    own_copy = pltpu.make_async_copy(tiles, own_buf, sem_own)
    past_copy.start()
    own_copy.start()
    barrier = pltpu.get_barrier_semaphore()
    for dy, dx in others:
        pl.semaphore_signal(barrier, inc=1, device_id=at(dy, dx), device_id_type=MESH)
    columns = [(row, lax.rem(col + d, COLS)) for d in range(1, COLS)]
    for device in columns:
        pl.semaphore_signal(barrier, inc=1, device_id=device, device_id_type=MESH)
    pool[pl.ds(HELP, 8)] = jnp.zeros((8, GROUP, GROUP), BF16)
    notices[row] = notice[...]
    fetch.wait()
    pl.semaphore_wait(barrier, len(others) + len(columns))
    notes = []
    for i, (dy, dx) in enumerate(others):
        note = pltpu.make_async_remote_copy(
            src_ref=notice,
            dst_ref=notices.at[row],
            send_sem=s_otx.at[i],
            recv_sem=s_orx.at[i],
            device_id=at(dy, dx),
            device_id_type=MESH,
        )
        note.start()
        notes.append(note)

    def hop(t, number):
        place = lax.rem(t, 2) * 4 + number
        return pltpu.make_async_remote_copy(
            src_ref=stage.at[place],
            dst_ref=landed.at[4 * t + number],
            send_sem=s_tx.at[place],
            recv_sem=s_rx.at[4 * t + number],
            device_id=links[number],
            device_id_type=MESH,
        )

    def keep(t, number):
        return pltpu.make_async_copy(
            landed.at[4 * t + number], out.at[4 * t + number], sem_out.at[4 * t + number]
        )

    def send(t):
        for number in range(4):
            stage[lax.rem(t, 2) * 4 + number] = pool[moves[4 * t + number]]
            hop(t, number).start()

    def take(t):
        for number in range(4):
            hop(t, number).wait_recv()
            keep(t, number).start()

    send(0)
    send(1)

    def save(k, place):
        return pltpu.make_async_copy(seg.at[place], sums.at[k], sem_seg.at[place])

    def own_fields(t):
        for i in range(4):
            k = 4 * (t - 2) + i

            @pl.when(t > 2)
            def _():
                save(k - 4, i).wait()

            first = tables[EVERY + 6, k]
            window = jnp.concatenate([past[first + p * COLS] for p in range(STEPS)], axis=1)
            term = jnp.dot(own_buf[tables[EVERY, k]], window, preferred_element_type=F32)
            seg[i] = seg[(i + 3) % 4] * tables[EVERY + 1, k].astype(F32) + term
            save(k, i).start()

    def advance(t):
        take(t - 2)
        for number in range(4):
            pool[HELP + 8 + 4 * (t - 2) + number] = landed[4 * (t - 2) + number]
            hop(t - 2, number).wait_send()
        send(t)

    def both(t):
        advance(t)
        own_fields(t)

    past[pl.ds(LAGS * COLS, 3 * COLS)] = jnp.zeros((3 * COLS, GROUP, RHS), BF16)
    seg[3] = jnp.zeros((GROUP, STEPS * RHS), F32)
    past_copy.wait()
    own_copy.wait()
    pl.loop(2, MIDDLE)(both)
    for note in notes:
        note.wait()
    for sender in range(ROWS):
        every_obs[pl.ds(sender, 1), :] = notices[sender, pl.ds(0, 1), :]
    peak[...] = jnp.max(notices[...], axis=0)
    peaks[col] = peak[...]
    tops = []
    for i, device in enumerate(columns):
        top = pltpu.make_async_remote_copy(
            src_ref=peak,
            dst_ref=peaks.at[col],
            send_sem=s_ptx.at[i],
            recv_sem=s_prx.at[i],
            device_id=device,
            device_id_type=MESH,
        )
        top.start()
        tops.append(top)
    pl.loop(MIDDLE, OWN // 4 + 2)(both)
    pl.loop(OWN // 4 + 2, rounds)(advance)
    for i in range(4):
        save(OWN - 4 + i, i).wait()
    for t in (rounds - 2, rounds - 1):
        take(t)
        for number in range(4):
            hop(t, number).wait_send()
    for top in tops:
        top.wait()
    most[...] = jnp.max(peaks[...], axis=0)

    @pl.loop(0, rounds)
    def _(t):
        for number in range(4):
            keep(t, number).wait()


def route(rounds, collective, moves, tables, help_tiles, history, tiles, notice):
    vmem = pl.BlockSpec(memory_space=pltpu.VMEM)
    hbm = pl.BlockSpec(memory_space=pl.ANY)
    dma = pltpu.SemaphoreType.DMA
    return pl.pallas_call(
        functools.partial(route_kernel, rounds),
        out_shape=(
            jax.ShapeDtypeStruct((4 * ROUNDS, GROUP, GROUP), BF16),
            jax.ShapeDtypeStruct((OWN, GROUP, STEPS * RHS), F32),
            jax.ShapeDtypeStruct((ROWS, 128), jnp.int32),
            jax.ShapeDtypeStruct((8, 128), jnp.int32),
        ),
        in_specs=[pl.BlockSpec(memory_space=pltpu.SMEM)] * 2 + [hbm] * 3 + [vmem],
        out_specs=(hbm, hbm, vmem, vmem),
        scratch_shapes=[
            pltpu.VMEM((HELP + 8 + 4 * rounds, GROUP, GROUP), BF16),
            pltpu.VMEM((4 * rounds, GROUP, GROUP), BF16),
            pltpu.VMEM((8, GROUP, GROUP), BF16),
            pltpu.VMEM((ROWS, 8, 128), jnp.int32),
            pltpu.VMEM((8, 128), jnp.int32),
            pltpu.VMEM((COLS, 8, 128), jnp.int32),
            pltpu.VMEM(((LAGS + 3) * COLS, GROUP, RHS), BF16),
            pltpu.VMEM((OWN, GROUP, GROUP), BF16),
            pltpu.VMEM((4, GROUP, STEPS * RHS), F32),
            dma,
            dma((4 * rounds,)),
            dma((8,)),
            dma((4 * rounds,)),
            dma((ROWS - 1,)),
            dma((ROWS - 1,)),
            dma((COLS - 1,)),
            dma((COLS - 1,)),
            dma,
            dma,
            dma((4,)),
        ],
        compiler_params=pltpu.CompilerParams(
            collective_id=collective, has_side_effects=True, vmem_limit_bytes=VMEM_LIMIT
        ),
    )(moves, tables, help_tiles, history, tiles, notice)


def history_kernel(
    aid, aid_obs, tables, history, sums, pool, out,
    listed, past, aid_buf, acc, own, sem_past, sem_aid, sem_own, sem_out,
):
    past_copies = history_copies(history, past, sem_past)
    for copy in past_copies:
        copy.start()
    empty = 4 * ROUNDS

    def aid_copy(t):
        return pltpu.make_async_copy(pool.at[t], aid_buf.at[t], sem_aid.at[t])

    def gather(t, count):
        here = (aid[t] != 0) & ((aid[t] & 15) == 0)

        @pl.when(here)
        def _():
            aid_copy(t).start()

        listed[count] = t
        return count + here.astype(jnp.int32)

    def own_copy(obs):
        return pltpu.make_async_copy(
            sums.at[tables[EVERY + 5, obs] - 1], own.at[obs], sem_own.at[obs]
        )

    def out_copy(obs):
        return pltpu.make_async_copy(acc.at[obs], out.at[obs], sem_out.at[obs])

    count = lax.fori_loop(0, 4 * ROUNDS, gather, 0)
    for i in range(4):
        listed[count + i] = empty

    @pl.loop(0, ROWS)
    def _(obs):
        @pl.when(tables[EVERY + 5, obs] > 0)
        def _():
            own_copy(obs).start()

    aid_buf[empty] = jnp.zeros((GROUP, GROUP), BF16)
    acc[...] = jnp.zeros(acc.shape, F32)
    past[:, :, pl.ds(LAGS * RHS, 3 * RHS)] = jnp.zeros((COLS, GROUP, 3 * RHS), BF16)
    for copy in past_copies:
        copy.wait()

    @pl.loop(0, count)
    def _(i):
        aid_copy(listed[i]).wait()

    @pl.loop(0, (count + 3) // 4)
    def _(group):
        for i in range(4):
            t = listed[4 * group + i]
            live = t < empty
            note = jnp.where(live, aid[jnp.minimum(t, empty - 1)], 5 << 16)
            obs = aid_obs[(note >> 9) & 15, (note >> 4) & 31]
            lag = ((note >> 16) & 7) + 3
            first = pl.multiple_of((LAGS - lag) * RHS, RHS)
            window = past[(note >> 13) & 7, :, pl.ds(first, STEPS * RHS)]
            acc[obs] += jnp.dot(aid_buf[t], window, preferred_element_type=F32)

    @pl.loop(0, ROWS)
    def _(obs):
        @pl.when(tables[EVERY + 5, obs] > 0)
        def _():
            own_copy(obs).wait()
            acc[obs] += own[obs]

        out_copy(obs).start()

    @pl.loop(0, ROWS)
    def _(obs):
        out_copy(obs).wait()


def history_fields(aid, aid_obs, tables, history, sums, pool):
    smem = pl.BlockSpec(memory_space=pltpu.SMEM)
    hbm = pl.BlockSpec(memory_space=pl.ANY)
    return pl.pallas_call(
        history_kernel,
        out_shape=jax.ShapeDtypeStruct((ROWS, GROUP, STEPS * RHS), F32),
        in_specs=[smem] * 3 + [hbm] * 3,
        out_specs=hbm,
        scratch_shapes=[
            pltpu.SMEM((4 * ROUNDS + 8,), jnp.int32),
            pltpu.VMEM((COLS, GROUP, (LAGS + 3) * RHS), BF16),
            pltpu.VMEM((4 * ROUNDS + 1, GROUP, GROUP), BF16),
            pltpu.VMEM((ROWS, GROUP, STEPS * RHS), F32),
            pltpu.VMEM((ROWS, GROUP, STEPS * RHS), F32),
            pltpu.SemaphoreType.DMA((LAGS,)),
            pltpu.SemaphoreType.DMA((4 * ROUNDS,)),
            pltpu.SemaphoreType.DMA((ROWS,)),
            pltpu.SemaphoreType.DMA((ROWS,)),
        ],
        compiler_params=pltpu.CompilerParams(vmem_limit_bytes=VMEM_LIMIT),
    )(aid, aid_obs, tables, history, sums, pool)


def march_kernel(
    slots1, slots23, tables, slab_hbm, tiles_hbm, inverse, excitation, out,
    slab, tiles, table, cur00, cur01, cur10, cur11, cur20, cur21, seg1, seg23, own, mine, right,
    tx1, rx1, tx2, rx2,
    sem_slab, sem_tiles, s_tx1, s_rx1, s_tx2, s_rx2, s_ztx, s_zrx, s_ctx, s_crx,
):
    row = lax.axis_index("src")
    col = lax.axis_index("obs")
    y, x = row // SIDE, lax.rem(row, SIDE)
    z, core = col // 2, lax.rem(col, 2)
    half, quarter = GROUP // 2, GROUP // 4
    cur = [[cur00, cur01], [cur10, cur11], [cur20, cur21]]
    lane = lax.broadcasted_iota(jnp.int32, (1, RHS), 1)
    in_half = [lane < RHS // 2, lane >= RHS // 2]
    here = (x, y)

    def turn(v, d):
        return lax.rem(v + d + SIDE, SIDE)

    def swap(value):
        return pltpu.roll(value, RHS // 2, 1)

    def plane(yy, xx):
        return (yy * SIDE + xx, col)

    partners = (
        [plane(y, turn(x, d)) for d in (1, 2, 3)]
        + [plane(turn(y, d), x) for d in (1, 2, 3)]
        + [(row, turn(z, d) * 2 + core) for d in (1, 2, 3)]
        + [(row, z * 2 + 1 - core)]
    )
    slab_copy = pltpu.make_async_copy(slab_hbm, slab, sem_slab)
    tiles_copy = pltpu.make_async_copy(tiles_hbm, tiles, sem_tiles)
    slab_copy.start()
    tiles_copy.start()
    barrier = pltpu.get_barrier_semaphore()
    for device in partners:
        pl.semaphore_signal(barrier, inc=1, device_id=device, device_id_type=MESH)
    table[...] = jnp.zeros(table.shape, BF16)
    seg1[0] = jnp.zeros((GROUP, RHS), F32)
    seg23[0] = jnp.zeros((GROUP, RHS), F32)
    slab_copy.wait()
    pl.semaphore_wait(barrier, len(partners))
    sent = []
    first, second, spread, across = {}, {}, {}, {}

    def products(seg, base, step, begin, end):
        def product(k, carry):
            term = jnp.dot(
                tiles[tables[base, k]],
                table[tables[base + 1 + step, k]],
                preferred_element_type=F32,
            )
            total = carry * tables[base + 1, k].astype(F32) + term
            seg[k + 1] = total
            return total

        lax.fori_loop(begin, end, product, seg[begin], unroll=4)

    def owner(part, other, along):
        return other * SIDE + along if part == 0 else along * SIDE + other

    def toward(part, along):
        return plane(y, along) if part == 0 else plane(along, x)

    def piece(step, part, obs):
        rows = pl.ds(part * half, half)
        value = slab[obs, rows, pl.ds(step * RHS, RHS)]
        if step >= 1:
            value = value + seg1[tables[LIST1 + 5, obs], rows, :]
        if step >= 2:
            value = value + seg23[tables[LIST23 + 5, obs], rows, :]
        return value

    def packed(step, h, part, along, pair):
        even = piece(step, part, owner(part, 2 * pair, along))
        odd = piece(step, part, owner(part, 2 * pair + 1, along))
        return jnp.where(in_half[h], even, swap(odd))

    def send_first(step, h):
        for d in (2, 1, 3):
            for part in (0, 1):
                along = turn(here[part], d)
                for pair in (0, 1):
                    tx1[step, h, part, d - 1, pair] = packed(step, h, part, along, pair).astype(BF16)
                copy = pltpu.make_async_remote_copy(
                    src_ref=tx1.at[step, h, part, d - 1],
                    dst_ref=rx1.at[step, h, part, d - 1],
                    send_sem=s_tx1.at[step, h, part, d - 1],
                    recv_sem=s_rx1.at[step, h, part, d - 1],
                    device_id=toward(part, along),
                    device_id_type=MESH,
                )
                copy.start()
                first[step, h, part, d] = copy
                sent.append(copy)
        for part in (0, 1):
            for pair in (0, 1):
                own[h, part, pair] = packed(step, h, part, here[part], pair)

    def send_second(step, h):
        for part in (0, 1):
            for d in (1, 3, 2):
                first[step, h, part, d].wait_recv()
            for pair in (0, 1):
                value = own[h, part, pair]
                for d in (1, 2, 3):
                    value = value + rx1[step, h, part, d - 1, pair].astype(F32)
                own[h, part, pair] = value

            def block(other):
                value = own[h, part, other // 2]
                value = jnp.where(lax.rem(other, 2) == 1, swap(value), value)
                return jnp.where(in_half[h], value[:quarter], swap(value[quarter:]))

            for d in (2, 1, 3):
                other = turn(here[1 - part], d)
                tx2[step, h, part, d - 1] = block(other)
                copy = pltpu.make_async_remote_copy(
                    src_ref=tx2.at[step, h, part, d - 1],
                    dst_ref=rx2.at[step, h, part, d - 1],
                    send_sem=s_tx2.at[step, h, part, d - 1],
                    recv_sem=s_rx2.at[step, h, part, d - 1],
                    device_id=toward(1 - part, other),
                    device_id_type=MESH,
                )
                copy.start()
                second[step, h, part, d] = copy
                sent.append(copy)
            mine[h, part] = block(here[1 - part])

    def solve(step, h):
        for part in (0, 1):
            value = mine[h, part]
            for d in (1, 3, 2):
                second[step, h, part, d].wait_recv()
                value = value + rx2[step, h, part, d - 1]
            for i, rows_value in enumerate((value, swap(value))):
                rows = pl.ds(part * half + i * quarter, quarter)
                right[rows, :] = excitation[step, 0, rows, :].astype(F32) - rows_value
        solved = jnp.dot(
            inverse[0], right[...], precision=lax.Precision.HIGHEST, preferred_element_type=F32
        )
        if step < STEPS - 1:
            now = cur[step][h]
            now[col] = jnp.where(in_half[h], solved[:half], swap(solved[half:])).astype(BF16)
            for e in (2, 1, 3):
                spread[step, h, e] = pltpu.make_async_remote_copy(
                    src_ref=now.at[col],
                    dst_ref=now.at[col],
                    send_sem=s_ztx.at[step, h, e - 1],
                    recv_sem=s_zrx.at[step, h, e - 1],
                    device_id=(row, turn(z, e) * 2 + core),
                    device_id_type=MESH,
                )
                spread[step, h, e].start()
                sent.append(spread[step, h, e])
            to_sibling(step, h, 0)
        if h == 0:
            out[step, 0] = solved.astype(BF16)
        else:
            out[step, 0] = jnp.where(in_half[h], solved, out[step, 0].astype(F32)).astype(BF16)

    def to_sibling(step, h, e):
        now = cur[step][h]
        block = turn(z, -e) * 2 + core
        across[step, h, e] = pltpu.make_async_remote_copy(
            src_ref=now.at[block],
            dst_ref=now.at[block],
            send_sem=s_ctx.at[step, h, e],
            recv_sem=s_crx.at[step, h, e],
            device_id=(row, z * 2 + 1 - core),
            device_id_type=MESH,
        )
        across[step, h, e].start()
        sent.append(across[step, h, e])

    def forward(step, h):
        for e in (1, 3, 2):
            spread[step, h, e].wait_recv()
            to_sibling(step, h, e)

    def collect(step, h):
        for e in (0, 1, 3, 2):
            across[step, h, e].wait_recv()

        @pl.loop(0, COLS)
        def _(g):
            value = cur[step][h][g].astype(F32)
            for i, part in enumerate((value, swap(value))):
                rows = pl.ds(i * half, half)
                if h == 1:
                    part = jnp.where(in_half[h], part, table[step * COLS + g, rows, :].astype(F32))
                table[step * COLS + g, rows, :] = part.astype(BF16)

    for step in range(STEPS):
        for h in (0, 1):
            if step:
                forward(step - 1, h)
                collect(step - 1, h)
                if step == 1 and h == 0:
                    tiles_copy.wait()
                products(seg1, LIST1, step, 0, slots1)
            send_first(step, h)
        early = 1 <= step < STEPS - 1
        if early:
            products(seg23, LIST23, step + 1, 0, slots23 // 2)
        for h in (0, 1):
            send_second(step, h)
        if early:
            products(seg23, LIST23, step + 1, slots23 // 2, slots23)
        for h in (0, 1):
            solve(step, h)
    for copy in sent:
        copy.wait_send()


def march(slots1, slots23, collective, tables, slab, tiles, inverse, excitation):
    hbm = pl.BlockSpec(memory_space=pl.ANY)
    vmem = pl.BlockSpec(memory_space=pltpu.VMEM)
    half = GROUP // 2
    dma = pltpu.SemaphoreType.DMA
    return pl.pallas_call(
        functools.partial(march_kernel, slots1, slots23),
        out_shape=jax.ShapeDtypeStruct((STEPS, 1, GROUP, RHS), BF16),
        in_specs=[pl.BlockSpec(memory_space=pltpu.SMEM)] + [hbm] * 2 + [vmem] * 2,
        out_specs=vmem,
        scratch_shapes=[
            pltpu.VMEM((ROWS, GROUP, STEPS * RHS), F32),
            pltpu.VMEM((OWN, GROUP, GROUP), BF16),
            pltpu.VMEM((3 * COLS + 1, GROUP, RHS), BF16),
        ]
        + [pltpu.VMEM((COLS, half, RHS), BF16)] * 6
        + [
            pltpu.VMEM((slots1 + 1, GROUP, RHS), F32),
            pltpu.VMEM((slots23 + 1, GROUP, RHS), F32),
            pltpu.VMEM((2, 2, 2, half, RHS), F32),
            pltpu.VMEM((2, 2, half // 2, RHS), F32),
            pltpu.VMEM((GROUP, RHS), F32),
            pltpu.VMEM((STEPS, 2, 2, 3, 2, half, RHS), BF16),
            pltpu.VMEM((STEPS, 2, 2, 3, 2, half, RHS), BF16),
            pltpu.VMEM((STEPS, 2, 2, 3, half // 2, RHS), F32),
            pltpu.VMEM((STEPS, 2, 2, 3, half // 2, RHS), F32),
            dma,
            dma,
            dma((STEPS, 2, 2, 3)),
            dma((STEPS, 2, 2, 3)),
            dma((STEPS, 2, 2, 3)),
            dma((STEPS, 2, 2, 3)),
            dma((STEPS - 1, 2, 3)),
            dma((STEPS - 1, 2, 3)),
            dma((STEPS - 1, 2, SIDE)),
            dma((STEPS - 1, 2, SIDE)),
        ],
        compiler_params=pltpu.CompilerParams(
            collective_id=collective, has_side_effects=True, vmem_limit_bytes=VMEM_LIMIT
        ),
    )(tables, slab, tiles, inverse, excitation)


def swap_help(help_tiles, help_obs, help_src, help_lag, row, column):
    src = lax.dynamic_index_in_dim(help_src.reshape(ROWS, COLS, HELP), column, 1, keepdims=False)
    lag = lax.dynamic_index_in_dim(help_lag.reshape(ROWS, COLS, HELP), column, 1, keepdims=False)
    target = src // COLS
    order = jnp.arange(HELP, dtype=jnp.int32)
    earlier = (target[:, :, None] == target[:, None, :]) & (order[None, None, :] < order[None, :, None])
    slot = jnp.sum(earlier.astype(jnp.int32), axis=2)
    mine_target = lax.dynamic_index_in_dim(target, row, 0, keepdims=False)
    mine_slot = lax.dynamic_index_in_dim(slot, row, 0, keepdims=False)
    place = jnp.arange(POOL, dtype=jnp.int32)
    sends = (mine_target * CAP + mine_slot)[None, :] == place[:, None]
    pick = jnp.sum(jnp.where(sends, order[None, :], 0), axis=1)
    tiles_out = jnp.take(help_tiles, pick, axis=0).reshape(ROWS, CAP, GROUP, GROUP)
    pool = lax.all_to_all(tiles_out, "src", split_axis=0, concat_axis=0, tiled=True)
    every_obs = lax.all_gather(help_obs, "src", axis=0, tiled=False)
    slots = jnp.arange(CAP, dtype=jnp.int32)
    got = (target[:, None, :] == row) & (slot[:, None, :] == slots[None, :, None])
    rows = jnp.arange(ROWS, dtype=jnp.int32)
    note = (((rows[:, None] << 5) | order[None, :]) << 4) | ((src % COLS) << 13) | ((lag - 3) << 16)
    aid = jnp.sum(jnp.where(got, note[:, None, :], 0), axis=2).reshape(-1)
    spare = 4 * ROUNDS - POOL
    pool = jnp.pad(pool.reshape(POOL, GROUP, GROUP), ((0, spare), (0, 0), (0, 0)))
    return pool, jnp.pad(every_obs, ((0, 0), (0, 128 - HELP))), jnp.pad(aid, (0, spare))


def on_device(
    history, tiles, tile_obs, tile_src, tile_lag,
    help_tiles, help_obs, help_src, help_lag, self_inverse, excitation,
):
    row = lax.axis_index("src")
    column = lax.axis_index("obs")
    moves, final, tables, notice, rounds = plan_routes(
        (help_src | (help_lag << 8)).reshape(ROWS * COLS, HELP).T,
        jnp.stack([tile_obs, tile_src, tile_lag]),
        jnp.stack([tile_obs, tile_src, tile_lag], axis=1),
        help_obs[None],
    )
    lane = row * COLS + column
    own_moves = lax.dynamic_index_in_dim(moves, lane, 1, keepdims=False)
    own_final = lax.dynamic_index_in_dim(final, lane, 1, keepdims=False)

    flat_history = history.reshape(LAGS * COLS, GROUP, RHS)

    def routed(count, collective):
        def run():
            pool, sums, every, most = route(
                count, collective, own_moves, tables, help_tiles, flat_history, tiles, notice
            )
            return pool, sums, every, own_final, most

        return run

    def general():
        most = lax.pmax(notice, ("src", "obs"))
        table = jnp.concatenate([history, jnp.zeros((3,) + history.shape[1:], BF16)])

        def add(total, entry):
            tile, joined, first = entry
            window = lax.dynamic_slice(
                table, (first // COLS, first % COLS, 0, 0), (STEPS, 1, GROUP, RHS)
            )[:, 0]
            term = jnp.einsum("ab,pbr->apr", tiles[tile], window, preferred_element_type=F32)
            total = jnp.where(joined != 0, total, 0.0) + term.reshape(GROUP, STEPS * RHS)
            return total, total

        entries = tuple(tables[EVERY + i] for i in (0, 1, 6))
        sums = lax.scan(add, jnp.zeros((GROUP, STEPS * RHS), F32), entries)[1]
        pool, every, aid = swap_help(help_tiles, help_obs, help_src, help_lag, row, column)
        return pool, sums, every, aid, most

    branches = [routed(count, 2 + i) for i, count in enumerate(CHOICES)] + [general]
    choice = sum((rounds[0] > count).astype(jnp.int32) for count in CHOICES)
    pool, sums, every_obs, aid, most = lax.switch(choice, branches)
    slab = history_fields(aid, every_obs, tables, history, sums, pool)

    def marched(slots1, slots23, collective):
        return lambda: march(
            slots1, slots23, collective, tables, slab, tiles, self_inverse, excitation
        )

    few = (most[1, 0] <= SLOTS1) & (most[2, 0] <= SLOTS23)
    return lax.cond(few, marched(SLOTS1, SLOTS23, 0), marched(OWN, OWN, 1))


def solution(mesh):
    placed = (
        P(None, "src", None, None),
        P(("src", "obs"), None, None),
        P(("src", "obs")),
        P(("src", "obs")),
        P(("src", "obs")),
        P(("src", "obs"), None, None),
        P(("src", "obs")),
        P(),
        P(),
        P(("src", "obs"), None, None),
        P(None, ("src", "obs"), None, None),
    )
    return jax.shard_map(
        on_device,
        mesh=mesh,
        in_specs=placed,
        out_specs=P(None, ("src", "obs"), None, None),
        check_vma=False,
    )
```
